128 devices in a mesh: mp: 2 (over core), tile: 64 (over y, z, x).
Axes of the slice: x: 4, y: 4, z: 4, core: 2. Of those that a mesh axis runs over, the one named last changes fastest.
Arguments:
- tracers: float32 [2, 4, 64, 1024, 512], P('mp', None, None, 'tile'), may hold values from -6 to 6
- diffusivity: float32 [2, 63, 1024, 512], P('mp', None, 'tile'), may hold values from 0.05 to 60
- conductance: float32 [2, 1024, 512], P('mp', 'tile'), may hold values from 0.2 to 4
- face_velocity: float32 [2, 64, 1024, 512], P('mp', None, 'tile'), may hold values from -0.3 to 0.3
- partner: int32 [2, 2, 1024, 512], P('mp', None, 'tile'), may hold values from 0 to 1023, as said below
- weight: int32 [2, 2, 1024, 512], P('mp', None, 'tile'), may hold values from 0 to 15, as said below
- sea_mask: int32 [1024, 512], P('tile'), may hold values from 0 to 1, as said below
Outputs:
- tracers_out: float32 [2, 4, 64, 1024, 512], P('mp', None, None, 'tile')
- surface_inflow: float32 [2, 4, 1024, 512], P('mp', None, 'tile')
The draws below stay inside these ranges and needn't reach their ends.
Inputs may be any that keep to these rules, and one draw needn't show every extreme that they name: `partner`: entry [m, k, x, y] names a column of the other component in the same row y that intersects column (x, y) of component m, at most 9 cells from x along the periodic X direction; each intersection is listed on both sides with the same weight. `weight`: intersection area in units of 1 / 16 of a cell; 0 exactly where the ocean column of the intersection is land. `sea_mask`: 1 marks an ocean column, 0 land.
All inputs are finite; a program needn't handle non-finite values.
Results may differ from the reference program's by a relative error of at most 0.00002.
Values sent between devices are 32-bit elements; how exact they have to be, the bound alone decides.
A program may use at most 192 MiB of HBM per device.

```python
import math
import jax
import jax.numpy as jnp
from jax import lax

CX = 16
NY = 512
LEV = 64
TRAC = 4
STEPS = 4
QUANT = 16
NXG = 1024


def coastline(key):
    coarse = jax.random.randint(jax.random.fold_in(key, 31), (NXG // 4, NY // 4), 0, 10)
    sea_cells = (coarse >= 3).astype(jnp.int32)
    sea_cells = jnp.repeat(jnp.repeat(sea_cells, 4, axis=0), 4, axis=1)
    return sea_cells.at[:, 0].set(1)


def intersection_tables(key):
    sea_cells = coastline(key)
    shifts = jax.random.randint(jax.random.fold_in(key, 32), (NY,), -(CX // 2), CX // 2 + 1)
    shifts = shifts.at[0].set(CX // 2)
    fractions = jax.random.randint(jax.random.fold_in(key, 33), (NY,), 1, QUANT)
    fractions = fractions.at[0].set(1)
    column_ids = jnp.arange(NXG, dtype=jnp.int32)[:, None]
    ocean_first = jnp.mod(column_ids + shifts[None], NXG)
    ocean_second = jnp.mod(ocean_first + 1, NXG)
    ocean_partner = jnp.stack([ocean_first, ocean_second])
    ocean_weight = jnp.stack([(QUANT - fractions)[None] * sea_cells, fractions[None] * sea_cells])
    atmos_near = jnp.mod(column_ids - shifts[None], NXG)
    atmos_far = jnp.mod(atmos_near - 1, NXG)
    atmos_partner = jnp.stack([atmos_near, atmos_far])
    atmos_weight = jnp.stack([(QUANT - fractions)[None] * jnp.take_along_axis(sea_cells, atmos_near, axis=0), fractions[None] * jnp.take_along_axis(sea_cells, atmos_far, axis=0)])
    partner_table = jnp.stack([atmos_partner, ocean_partner]).astype(jnp.int32)
    weight_table = jnp.stack([atmos_weight, ocean_weight]).astype(jnp.int32)
    return (partner_table, weight_table, sea_cells.astype(jnp.int32))


def draw_partner(key, part):
    return intersection_tables(key)[0]


def draw_weight(key, part):
    return intersection_tables(key)[1]


def draw_sea_mask(key, part):
    return intersection_tables(key)[2]


def draw_diffusivity(key, part):
    key = jax.random.fold_in(key, 41)
    shape_all = (2, LEV - 1, NXG, NY)
    strong_low = 15.0
    share_of_four = 2
    background = jnp.exp(jax.random.uniform(jax.random.fold_in(key, 1), shape_all, jnp.float32, math.log(0.05), math.log(5.0)))
    strong = jnp.exp(jax.random.uniform(jax.random.fold_in(key, 2), shape_all, jnp.float32, math.log(strong_low), math.log(60.0)))
    flagged = jax.random.randint(jax.random.fold_in(key, 3), (2, NXG // 4, NY // 4), 0, 4) < share_of_four
    layer_depth = jax.random.randint(jax.random.fold_in(key, 4), (2, NXG // 4, NY // 4), LEV // 3, LEV)
    layer_depth = jnp.where(flagged, layer_depth, 0)
    layer_depth = jnp.repeat(jnp.repeat(layer_depth, 4, axis=1), 4, axis=2)
    levels = jnp.arange(LEV - 1, dtype=jnp.int32)[None, :, None, None]
    mixed = levels >= LEV - 1 - layer_depth[:, None]
    return jnp.where(mixed, strong, background).astype(jnp.float32)


def steps_of(key, extent, pieces, least, high):
    level = 1.0
    for axis_at, blocks in pieces:
        draws = jax.random.uniform(jax.random.fold_in(jax.random.fold_in(key, 6), axis_at), (blocks,), jnp.float32, least / len(pieces), high / len(pieces))
        level = level * jnp.repeat(jnp.exp(draws), extent[axis_at] // blocks).reshape((-1,) + (1,) * (len(extent) - 1 - axis_at))
    return level


def scatter_about(key, shape, deviation, limit, shards=(), kind=jnp.bfloat16):
    drawn = deviation * jax.random.normal(key, shape, jnp.float32)
    if shards:
        drawn = drawn * steps_of(key, shape, shards, -0.22, 0.18)
    return jnp.clip(drawn, -limit, limit).astype(kind)


def setup_inputs(seed: int = 0) -> dict:
    arg_keys = jax.random.split(jax.random.key(seed), 8)
    tracers = scatter_about(arg_keys[0], (2, TRAC, LEV, NXG, NY), 1.0, 6.0, ((0, 2), (3, 64)), jnp.float32)
    diffusivity = draw_diffusivity(jax.random.fold_in(arg_keys[7], 71), 0)
    conductance = jnp.clip(jnp.exp(math.log(4.0) - 2.9957323 * jax.random.uniform(arg_keys[2], (2, NXG, NY), jnp.float32) ** steps_of(arg_keys[2], (2, NXG, NY), ((0, 2), (1, 64)), -0.2, 0.2)), 0.2, 4.0)
    face_velocity = jnp.clip(jax.random.uniform(arg_keys[3], (2, LEV, NXG, NY), jnp.float32, -0.3, 0.3) * steps_of(arg_keys[3], (2, LEV, NXG, NY), ((0, 2), (2, 64)), -0.4, 0.0), -0.3, 0.3)
    partner = draw_partner(jax.random.fold_in(arg_keys[7], 71), 0)
    weight = draw_weight(jax.random.fold_in(arg_keys[7], 71), 0)
    sea_mask = draw_sea_mask(jax.random.fold_in(arg_keys[7], 71), 0)
    return {"tracers": tracers, "diffusivity": diffusivity, "conductance": conductance, "face_velocity": face_velocity, "partner": partner, "weight": weight, "sea_mask": sea_mask}


diffusion_nu = 0.12


def down_sweep(previous, coupling):
    zero_row = jnp.zeros_like(coupling[:, :1])
    lower_side = jnp.concatenate([zero_row, coupling], axis=1)
    upper_side = jnp.concatenate([coupling, zero_row], axis=1)

    def eliminate(state_in, inputs):
        ratio_prev, part_prev, pivot_prev = state_in
        source, low_side, high_side = inputs
        pivot_now = 1.0 + low_side + high_side - low_side * ratio_prev
        part_now = (source + low_side[:, None] * part_prev) / pivot_now[:, None]
        ratio_now = high_side / pivot_now
        return (ratio_now, part_now, pivot_now), (part_now, ratio_now)

    initial = (jnp.zeros_like(coupling[:, 0]), jnp.zeros_like(previous[:, :, 0]), jnp.ones_like(coupling[:, 0]))
    inputs = (jnp.moveaxis(previous, 2, 0), jnp.moveaxis(lower_side, 1, 0), jnp.moveaxis(upper_side, 1, 0))
    finals, (partials, ratios) = lax.scan(eliminate, initial, inputs, unroll=8)
    return partials, ratios, finals[2]


def up_sweep(partials, ratios, surface):
    def back_substitute(upper_value, inputs):
        part_now, ratio_now = inputs
        value_now = part_now + ratio_now[:, None] * upper_value
        return value_now, value_now

    _, lowers = lax.scan(back_substitute, surface, (partials[:-1], ratios[:-1]), reverse=True, unroll=8)
    column = jnp.concatenate([lowers, surface[None]], axis=0)
    return jnp.moveaxis(column, 0, 2)


def surface_flux(own_terms, peer_terms, weight):
    own_value = own_terms[:, :-2]
    own_slope = own_terms[:, -2]
    own_conduct = own_terms[:, -1]
    peer_value = peer_terms[:, :-2]
    peer_slope = peer_terms[:, -2]
    peer_conduct = peer_terms[:, -1]
    series = own_conduct[:, None] * peer_conduct / (own_conduct[:, None] + peer_conduct)
    denominator = 1.0 + series * (own_slope[:, None] + peer_slope)
    outflow = series[:, None] * (own_value[:, :, None] - peer_value) / denominator[:, None]
    return -jnp.sum(weight.astype(jnp.float32)[:, None] * outflow, axis=2) / QUANT


def advance(field_in, velocity, openness):
    open_east = (openness[:, :-1] * openness[:, 1:])[:, None, None]
    east_speed = velocity[:, None, :, :-1, :]
    left_side = field_in[..., :-1, :]
    right_side = field_in[..., 1:, :]
    east_flux = open_east * (jnp.maximum(east_speed, 0.0) * left_side + jnp.minimum(east_speed, 0.0) * right_side - diffusion_nu * (right_side - left_side))
    open_north = (openness[:, :, :-1] * openness[:, :, 1:])[:, None, None]
    north_flux = -diffusion_nu * open_north * (field_in[..., 1:] - field_in[..., :-1])
    north_padded = jnp.pad(north_flux, [(0, 0), (0, 0), (0, 0), (0, 0), (1, 1)])
    change_x = east_flux[..., 1:, :] - east_flux[..., :-1, :]
    change_y = north_padded[..., 1:] - north_padded[..., :-1]
    return field_in[..., 1:-1, :] - change_x - change_y[..., 1:-1, :]


def wrap_periodic(values):
    return jnp.concatenate([values[..., -1:, :], values, values[..., :1, :]], axis=-2)


def reference(tracers, diffusivity, conductance, face_velocity, partner, weight, sea_mask):
    partials, ratios, pivots = down_sweep(tracers, diffusivity)
    slopes = 1.0 / pivots
    own_terms = jnp.concatenate([partials[-1], slopes[:, None], conductance[:, None]], axis=1)
    other_terms = own_terms[::-1]
    shape_all = (2, TRAC + 2, 2, NXG, NY)
    peer_terms = jnp.take_along_axis(jnp.broadcast_to(other_terms[:, :, None], shape_all), jnp.broadcast_to(partner[:, None], shape_all), axis=3)
    inflow = surface_flux(own_terms, peer_terms, weight)
    surface = partials[-1] + slopes[:, None] * inflow
    columns = up_sweep(partials, ratios, surface)
    openness = jnp.stack([jnp.ones((NXG, NY), jnp.float32), sea_mask.astype(jnp.float32)])
    for section_index in range(STEPS):
        columns = advance(wrap_periodic(columns), wrap_periodic(face_velocity), wrap_periodic(openness))
    return columns, inflow
```

```python
import functools

import jax
import jax.numpy as jnp
from jax import lax
from jax.experimental import pallas as pl
from jax.experimental.pallas import tpu as pltpu
from jax.sharding import PartitionSpec as P

STEPS = 4
QUANT = 16
CHUNK = 8
REACH = 9

diffusion_nu = 0.12
MESH = pl.DeviceIdType.MESH


def kernel(
    count,
    tracers,
    diffusivity,
    conductance,
    velocity,
    partner,
    weight,
    sea_mask,
    out,
    inflow_out,
    q,
    lower,
    ratio,
    inverse,
    speed,
    keep,
    east,
    west,
    from_left,
    from_right,
    speed_left,
    mask_own,
    mask_left,
    mask_right,
    terms,
    wide,
    partner_own,
    weight_own,
    inflow,
    load_sem,
    tracer_sem,
    store_sem,
    misc_send,
    misc_recv,
    edge_send,
    edge_recv,
):
    _, trac, lev, width, rows = q.shape
    chunks = lev // CHUNK
    component = lax.axis_index("mp")
    tile = lax.axis_index("tile")
    other = 1 - component
    right = lax.rem(tile + 1, count)
    left = lax.rem(tile + count - 1, count)
    half = width // 2

    def chunk_load(c):
        part = pl.ds(c * CHUNK, CHUNK)
        return pltpu.make_async_copy(tracers.at[0, :, part], q.at[0, :, part], tracer_sem.at[c])

    def chunk_store(c):
        part = pl.ds(c * CHUNK, CHUNK)
        return pltpu.make_async_copy(q.at[0, :, part], out.at[0, :, part], store_sem.at[c])

    loads = [
        pltpu.make_async_copy(source, target, load_sem.at[i])
        for i, (source, target) in enumerate(
            [
                (diffusivity.at[0], lower.at[pl.ds(0, lev - 1)]),
                (conductance.at[0], terms.at[trac + 1]),
                (sea_mask, mask_own),
                (velocity.at[0], speed),
                (partner.at[0], partner_own),
                (weight.at[0], weight_own),
            ]
        )
    ]
    loads[0].start()
    for c in range(chunks):
        chunk_load(c).start()
    for load in loads[1:]:
        load.start()

    barrier = pltpu.get_barrier_semaphore()
    peers = [(component, left), (component, right), (other, tile), (other, left), (other, right)]
    for peer in peers:
        pl.semaphore_signal(barrier, inc=1, device_id=peer, device_id_type=MESH)
    pl.semaphore_wait(barrier, len(peers))

    def send(index, source, target, peer):
        return pltpu.make_async_remote_copy(
            src_ref=source,
            dst_ref=target,
            send_sem=misc_send.at[index],
            recv_sem=misc_recv.at[index],
            device_id=peer,
            device_id_type=MESH,
        )

    early = [
        send(0, velocity.at[0, :, width - 1], speed_left, (component, right)),
        send(1, sea_mask.at[pl.ds(half, half)], mask_left, (component, right)),
        send(2, sea_mask.at[pl.ds(0, half)], mask_right, (component, left)),
    ]
    exchange = [
        send(3, terms, wide.at[:, pl.ds(width, width)], (other, tile)),
        send(4, terms.at[:, pl.ds(half, half)], wide.at[:, pl.ds(half, half)], (other, right)),
        send(5, terms.at[:, half - 1], wide.at[:, half - 1], (other, right)),
        send(6, terms.at[:, pl.ds(0, half)], wide.at[:, pl.ds(2 * width, half)], (other, left)),
        send(7, terms.at[:, half], wide.at[:, 2 * width + half], (other, left)),
    ]
    for copy in early:
        copy.start()

    def edges(s, c):
        part = pl.ds(c * CHUNK, CHUNK)
        field = lax.rem(s, 2)
        return [
            pltpu.make_async_remote_copy(
                src_ref=q.at[field, :, part, column],
                dst_ref=target.at[s, c],
                send_sem=edge_send.at[side, s, c],
                recv_sem=edge_recv.at[side, s, c],
                device_id=(component, peer),
                device_id_type=MESH,
            )
            for side, (column, target, peer) in enumerate(
                [(width - 1, from_left, right), (0, from_right, left)]
            )
        ]

    loads[0].wait()
    zero = jnp.zeros((width, rows), jnp.float32)
    lower[lev - 1] = zero

    def factor(l, carry):
        low, ratio_prev = carry
        high = lower[l]
        inv = 1.0 / (1.0 + low + high - low * ratio_prev)
        ratio_now = high * inv
        inverse[l] = inv
        lower[l] = low * inv
        ratio[l] = ratio_now
        return high, ratio_now

    lax.fori_loop(0, lev, factor, (zero, zero))
    slope = inverse[lev - 1]
    ratio[lev - 1] = slope

    def down_chunk(c, carry):
        chunk_load(c).wait()

        def down(k, partial):
            l = c * CHUNK + k
            low = lower[l]
            inv = inverse[l]
            now = tuple(q[0, t, l] * inv + low * partial[t] for t in range(trac))
            for t in range(trac):
                q[0, t, l] = now[t]
            return now

        return lax.fori_loop(0, CHUNK, down, carry)

    finals = lax.fori_loop(0, chunks, down_chunk, (zero,) * trac)
    for t in range(trac):
        terms[t] = finals[t]
    terms[trac] = slope
    loads[1].wait()
    for copy in exchange:
        copy.start()

    for load in loads[2:]:
        load.wait()
    for copy in early:
        copy.wait_recv()
    row = lax.broadcasted_iota(jnp.int32, (width, rows), 0)
    lane = lax.broadcasted_iota(jnp.int32, (width, rows), 1)
    first = row == 0
    last = row == width - 1

    def openness_of(mask):
        return jnp.where(component == 1, mask.astype(jnp.float32), jnp.ones(mask.shape, jnp.float32))

    openness = openness_of(mask_own[...])
    open_right = openness_of(mask_right[pl.ds(0, 1), :])
    open_left = openness_of(mask_left[pl.ds(half - 1, 1), :])
    open_east = openness * jnp.where(last, open_right, pltpu.roll(openness, width - 1, 0))
    open_west = openness * jnp.where(first, open_left, pltpu.roll(openness, 1, 0))
    north = jnp.where(lane == rows - 1, 0.0, diffusion_nu * openness * pltpu.roll(openness, rows - 1, 1))
    south = jnp.where(lane == 0, 0.0, diffusion_nu * openness * pltpu.roll(openness, 1, 1))

    def coefficients(l, _):
        here = speed[l]
        before = jnp.where(first, speed_left[pl.ds(l, 1), :], pltpu.roll(here, 1, 0))
        keep[l] = (
            1.0
            - north
            - south
            - open_east * (jnp.maximum(here, 0.0) + diffusion_nu)
            + open_west * (jnp.minimum(before, 0.0) - diffusion_nu)
        )
        east[l] = open_east * (diffusion_nu - jnp.minimum(here, 0.0))
        west[l] = open_west * (jnp.maximum(before, 0.0) + diffusion_nu)
        return 0

    lax.fori_loop(0, lev, coefficients, 0)

    for copy in exchange:
        copy.wait_recv()
    columns = count * width
    lanes = 128

    def surface(j, _):
        part = pl.ds(pl.multiple_of(j * lanes, lanes), lanes)
        for h in range(2):
            own_rows = pl.ds(h * half, half)
            place = tile * width + h * half + lax.broadcasted_iota(jnp.int32, (half, lanes), 0)
            own = [terms[ch, own_rows, part] for ch in range(trac + 2)]
            total = [jnp.zeros((half, lanes), jnp.float32) for _ in range(trac)]
            distance = [
                lax.rem(partner_own[k, own_rows, part] - place + (REACH + columns), columns)
                for k in range(2)
            ]
            peer = [[jnp.zeros((half, lanes), jnp.float32)] * (trac + 2) for k in range(2)]
            for offset in range(2 * REACH + 1):
                begin = width - REACH + offset + h * half
                hit = [distance[k] == offset for k in range(2)]
                for ch in range(trac + 2):
                    window = wide[ch, pl.ds(begin, half), part]
                    for k in range(2):
                        peer[k][ch] = jnp.where(hit[k], window, peer[k][ch])
            for k in range(2):
                series = own[trac + 1] * peer[k][trac + 1] / (own[trac + 1] + peer[k][trac + 1])
                scale = (
                    weight_own[k, own_rows, part].astype(jnp.float32)
                    * series
                    / (1.0 + series * (own[trac] + peer[k][trac]))
                )
                for t in range(trac):
                    total[t] = total[t] + scale * (own[t] - peer[k][t])
            for t in range(trac):
                inflow[t, own_rows, part] = total[t] * (-1.0 / QUANT)
        return 0

    lax.fori_loop(0, rows // lanes, surface, 0)
    store_inflow = pltpu.make_async_copy(inflow, inflow_out.at[0], load_sem.at[0])
    store_inflow.start()

    def up_chunk(i, carry):
        c = chunks - 1 - i

        def up(k, above):
            l = c * CHUNK + CHUNK - 1 - k
            slant = ratio[l]
            now = tuple(q[0, t, l] + slant * above[t] for t in range(trac))
            for t in range(trac):
                q[0, t, l] = now[t]
            return now

        carry = lax.fori_loop(0, CHUNK, up, carry)
        for copy in edges(0, c):
            copy.start()
        return carry

    lax.fori_loop(0, chunks, up_chunk, tuple(inflow[t] for t in range(trac)))

    def unit(i, _):
        s = i // chunks
        c = chunks - 1 - lax.rem(i, chunks)
        field = lax.rem(s, 2)

        @pl.when(s > 0)
        def _():
            for copy in edges(s - 1, c):
                copy.wait_send()

        for copy in edges(s, c):
            copy.wait_recv()

        def level(k, _):
            l = c * CHUNK + k
            keep_l = keep[l]
            east_l = east[l]
            west_l = west[l]
            for t in range(trac):
                here = q[field, t, l]
                after = jnp.where(last, from_right[s, c, t, pl.ds(k, 1), :], pltpu.roll(here, width - 1, 0))
                before = jnp.where(first, from_left[s, c, t, pl.ds(k, 1), :], pltpu.roll(here, 1, 0))
                q[1 - field, t, l] = (
                    keep_l * here
                    + east_l * after
                    + west_l * before
                    + north * pltpu.roll(here, rows - 1, 1)
                    + south * pltpu.roll(here, 1, 1)
                )
            return 0

        lax.fori_loop(0, CHUNK, level, 0)

        @pl.when(s < STEPS - 1)
        def _():
            for copy in edges(s + 1, c):
                copy.start()

        @pl.when(s == STEPS - 1)
        def _():
            chunk_store(c).start()

        return 0

    lax.fori_loop(0, STEPS * chunks, unit, 0)

    for c in range(chunks):
        for copy in edges(STEPS - 1, c):
            copy.wait_send()
        chunk_store(c).wait()
    for copy in early + exchange:
        copy.wait_send()
    store_inflow.wait()


def per_device(count, tracers, diffusivity, conductance, face_velocity, partner, weight, sea_mask):
    _, trac, lev, width, rows = tracers.shape
    chunks = lev // CHUNK
    full = (lev, width, rows)
    flat = (width, rows)
    anywhere = pl.BlockSpec(memory_space=pl.ANY)
    edge = (STEPS, chunks, trac, CHUNK, rows)
    dma = pltpu.SemaphoreType.DMA
    real = jnp.float32
    return pl.pallas_call(
        functools.partial(kernel, count),
        out_shape=(
            jax.ShapeDtypeStruct(tracers.shape, real),
            jax.ShapeDtypeStruct((1, trac, width, rows), real),
        ),
        in_specs=[anywhere] * 7,
        out_specs=(anywhere, anywhere),
        scratch_shapes=[
            pltpu.VMEM((2, trac) + full, real),
            pltpu.VMEM(full, real),
            pltpu.VMEM(full, real),
            pltpu.VMEM(full, real),
            pltpu.VMEM(full, real),
            pltpu.VMEM(full, real),
            pltpu.VMEM(full, real),
            pltpu.VMEM(full, real),
            pltpu.VMEM(edge, real),
            pltpu.VMEM(edge, real),
            pltpu.VMEM((lev, rows), real),
            pltpu.VMEM(flat, jnp.int32),
            pltpu.VMEM((width // 2, rows), jnp.int32),
            pltpu.VMEM((width // 2, rows), jnp.int32),
            pltpu.VMEM((trac + 2,) + flat, real),
            pltpu.VMEM((trac + 2, 3 * width, rows), real),
            pltpu.VMEM((2,) + flat, jnp.int32),
            pltpu.VMEM((2,) + flat, jnp.int32),
            pltpu.VMEM((trac,) + flat, real),
            dma((6,)),
            dma((chunks,)),
            dma((chunks,)),
            dma((8,)),
            dma((8,)),
            dma((2, STEPS, chunks)),
            dma((2, STEPS, chunks)),
        ],
        compiler_params=pltpu.CompilerParams(
            collective_id=0, has_side_effects=True, vmem_limit_bytes=56 * 1024 * 1024
        ),
        name="coupled_step",
    )(tracers, diffusivity, conductance, face_velocity, partner, weight, sea_mask)


def solution(mesh):
    in_specs = (
        P("mp", None, None, "tile", None),
        P("mp", None, "tile", None),
        P("mp", "tile", None),
        P("mp", None, "tile", None),
        P("mp", None, "tile", None),
        P("mp", None, "tile", None),
        P("tile", None),
    )
    out_specs = (P("mp", None, None, "tile", None), P("mp", None, "tile", None))
    return jax.shard_map(
        functools.partial(per_device, mesh.shape["tile"]),
        mesh=mesh,
        in_specs=in_specs,
        out_specs=out_specs,
        check_vma=False,
    )
```

```python
import functools

import jax
import jax.numpy as jnp
from jax import lax
from jax.experimental import pallas as pl
from jax.experimental.pallas import tpu as pltpu
from jax.sharding import PartitionSpec as P

STEPS = 4
QUANT = 16
CHUNK = 8
REACH = 9

diffusion_nu = 0.12
MESH = pl.DeviceIdType.MESH


def kernel(
    count,
    tracers,
    diffusivity,
    conductance,
    velocity,
    partner,
    weight,
    sea_mask,
    out,
    inflow_out,
    spare,
    lower,
    ratio,
    inverse,
    speed,
    keep,
    east,
    west,
    from_left,
    from_right,
    speed_left,
    mask_own,
    mask_left,
    mask_right,
    terms,
    wide,
    partner_own,
    weight_own,
    load_sem,
    tracer_sem,
    misc_send,
    misc_recv,
    edge_send,
    edge_recv,
):
    _, trac, lev, width, rows = out.shape
    field = out.at[0]
    inflow = inflow_out.at[0]
    fields = (field, spare)
    chunks = lev // CHUNK
    component = lax.axis_index("mp")
    tile = lax.axis_index("tile")
    other = 1 - component
    right = lax.rem(tile + 1, count)
    left = lax.rem(tile + count - 1, count)
    half = width // 2

    def chunk_load(c):
        part = pl.ds(c * CHUNK, CHUNK)
        return pltpu.make_async_copy(tracers.at[0, :, part], field.at[:, part], tracer_sem.at[c])

    loads = [
        pltpu.make_async_copy(source, target, load_sem.at[i])
        for i, (source, target) in enumerate(
            [
                (diffusivity.at[0], lower.at[pl.ds(0, lev - 1)]),
                (conductance.at[0], terms.at[trac + 1]),
                (sea_mask, mask_own),
                (velocity.at[0], speed),
                (partner.at[0], partner_own),
                (weight.at[0], weight_own),
            ]
        )
    ]
    loads[0].start()
    for c in range(chunks):
        chunk_load(c).start()
    for load in loads[1:]:
        load.start()

    barrier = pltpu.get_barrier_semaphore()
    peers = [(component, left), (component, right), (other, tile), (other, left), (other, right)]
    for peer in peers:
        pl.semaphore_signal(barrier, inc=1, device_id=peer, device_id_type=MESH)
    pl.semaphore_wait(barrier, len(peers))

    def send(index, source, target, peer):
        return pltpu.make_async_remote_copy(
            src_ref=source,
            dst_ref=target,
            send_sem=misc_send.at[index],
            recv_sem=misc_recv.at[index],
            device_id=peer,
            device_id_type=MESH,
        )

    early = [
        send(0, velocity.at[0, :, width - 1], speed_left, (component, right)),
        send(1, sea_mask.at[pl.ds(half, half)], mask_left, (component, right)),
        send(2, sea_mask.at[pl.ds(0, half)], mask_right, (component, left)),
    ]
    exchange = [
        send(3, terms, wide.at[:, pl.ds(width, width)], (other, tile)),
        send(4, terms.at[:, pl.ds(half, half)], wide.at[:, pl.ds(half, half)], (other, right)),
        send(5, terms.at[:, half - 1], wide.at[:, half - 1], (other, right)),
        send(6, terms.at[:, pl.ds(0, half)], wide.at[:, pl.ds(2 * width, half)], (other, left)),
        send(7, terms.at[:, half], wide.at[:, 2 * width + half], (other, left)),
    ]
    for copy in early:
        copy.start()

    def edges(s, c):
        part = pl.ds(c * CHUNK, CHUNK)
        return [
            pltpu.make_async_remote_copy(
                src_ref=fields[s % 2].at[:, part, column],
                dst_ref=target.at[s, c],
                send_sem=edge_send.at[side, s, c],
                recv_sem=edge_recv.at[side, s, c],
                device_id=(component, peer),
                device_id_type=MESH,
            )
            for side, (column, target, peer) in enumerate(
                [(width - 1, from_left, right), (0, from_right, left)]
            )
        ]

    loads[0].wait()
    zero = jnp.zeros((width, rows), jnp.float32)
    lower[lev - 1] = zero

    def factor(l, carry):
        low, ratio_prev = carry
        high = lower[l]
        inv = 1.0 / (1.0 + low + high - low * ratio_prev)
        ratio_now = high * inv
        inverse[l] = inv
        lower[l] = low * inv
        ratio[l] = ratio_now
        return high, ratio_now

    lax.fori_loop(0, lev, factor, (zero, zero))
    slope = inverse[lev - 1]
    ratio[lev - 1] = slope

    def down_chunk(c, carry):
        chunk_load(c).wait()

        def down(k, partial):
            l = c * CHUNK + k
            low = lower[l]
            inv = inverse[l]
            now = tuple(field[t, l] * inv + low * partial[t] for t in range(trac))
            for t in range(trac):
                field[t, l] = now[t]
            return now

        return lax.fori_loop(0, CHUNK, down, carry)

    finals = lax.fori_loop(0, chunks, down_chunk, (zero,) * trac)
    for t in range(trac):
        terms[t] = finals[t]
    terms[trac] = slope
    loads[1].wait()
    for copy in exchange:
        copy.start()

    for load in loads[2:]:
        load.wait()
    for copy in early:
        copy.wait_recv()
    row = lax.broadcasted_iota(jnp.int32, (width, rows), 0)
    lane = lax.broadcasted_iota(jnp.int32, (width, rows), 1)
    first = row == 0
    last = row == width - 1

    def openness_of(mask):
        return jnp.where(component == 1, mask.astype(jnp.float32), jnp.ones(mask.shape, jnp.float32))

    openness = openness_of(mask_own[...])
    open_right = openness_of(mask_right[pl.ds(0, 1), :])
    open_left = openness_of(mask_left[pl.ds(half - 1, 1), :])
    open_east = openness * jnp.where(last, open_right, pltpu.roll(openness, width - 1, 0))
    open_west = openness * jnp.where(first, open_left, pltpu.roll(openness, 1, 0))
    north = jnp.where(lane == rows - 1, 0.0, diffusion_nu * openness * pltpu.roll(openness, rows - 1, 1))
    south = jnp.where(lane == 0, 0.0, diffusion_nu * openness * pltpu.roll(openness, 1, 1))

    def coefficients(l, _):
        here = speed[l]
        before = jnp.where(first, speed_left[pl.ds(l, 1), :], pltpu.roll(here, 1, 0))
        keep[l] = (
            1.0
            - north
            - south
            - open_east * (jnp.maximum(here, 0.0) + diffusion_nu)
            + open_west * (jnp.minimum(before, 0.0) - diffusion_nu)
        )
        east[l] = open_east * (diffusion_nu - jnp.minimum(here, 0.0))
        west[l] = open_west * (jnp.maximum(before, 0.0) + diffusion_nu)
        return 0

    lax.fori_loop(0, lev, coefficients, 0)

    for copy in exchange:
        copy.wait_recv()
    columns = count * width
    lanes = 128

    def surface(j, _):
        part = pl.ds(pl.multiple_of(j * lanes, lanes), lanes)
        for h in range(2):
            own_rows = pl.ds(h * half, half)
            place = tile * width + h * half + lax.broadcasted_iota(jnp.int32, (half, lanes), 0)
            own = [terms[ch, own_rows, part] for ch in range(trac + 2)]
            total = [jnp.zeros((half, lanes), jnp.float32) for _ in range(trac)]
            distance = [
                lax.rem(partner_own[k, own_rows, part] - place + (REACH + columns), columns)
                for k in range(2)
            ]
            peer = [[jnp.zeros((half, lanes), jnp.float32)] * (trac + 2) for k in range(2)]
            for offset in range(2 * REACH + 1):
                begin = width - REACH + offset + h * half
                hit = [distance[k] == offset for k in range(2)]
                for ch in range(trac + 2):
                    window = wide[ch, pl.ds(begin, half), part]
                    for k in range(2):
                        peer[k][ch] = jnp.where(hit[k], window, peer[k][ch])
            for k in range(2):
                series = own[trac + 1] * peer[k][trac + 1] / (own[trac + 1] + peer[k][trac + 1])
                scale = (
                    weight_own[k, own_rows, part].astype(jnp.float32)
                    * series
                    / (1.0 + series * (own[trac] + peer[k][trac]))
                )
                for t in range(trac):
                    total[t] = total[t] + scale * (own[t] - peer[k][t])
            for t in range(trac):
                inflow[t, own_rows, part] = total[t] * (-1.0 / QUANT)
        return 0

    lax.fori_loop(0, rows // lanes, surface, 0)

    def up_chunk(i, carry):
        c = chunks - 1 - i

        def up(k, above):
            l = c * CHUNK + CHUNK - 1 - k
            slant = ratio[l]
            now = tuple(field[t, l] + slant * above[t] for t in range(trac))
            for t in range(trac):
                field[t, l] = now[t]
            return now

        carry = lax.fori_loop(0, CHUNK, up, carry)
        for copy in edges(0, c):
            copy.start()
        return carry

    lax.fori_loop(0, chunks, up_chunk, tuple(inflow[t] for t in range(trac)))

    def step(s):
        source, target = fields[s % 2], fields[(s + 1) % 2]

        def unit(i, _):
            c = chunks - 1 - i
            if s > 0:
                for copy in edges(s - 1, c):
                    copy.wait_send()
            for copy in edges(s, c):
                copy.wait_recv()

            def level(k, _):
                l = c * CHUNK + k
                keep_l = keep[l]
                east_l = east[l]
                west_l = west[l]
                for t in range(trac):
                    here = source[t, l]
                    after = jnp.where(last, from_right[s, c, t, pl.ds(k, 1), :], pltpu.roll(here, width - 1, 0))
                    before = jnp.where(first, from_left[s, c, t, pl.ds(k, 1), :], pltpu.roll(here, 1, 0))
                    target[t, l] = (
                        keep_l * here
                        + east_l * after
                        + west_l * before
                        + north * pltpu.roll(here, rows - 1, 1)
                        + south * pltpu.roll(here, 1, 1)
                    )
                return 0

            lax.fori_loop(0, CHUNK, level, 0, unroll=True)
            if s < STEPS - 1:
                for copy in edges(s + 1, c):
                    copy.start()
            return 0

        lax.fori_loop(0, chunks, unit, 0)

    for s in range(STEPS):
        step(s)

    for c in range(chunks):
        for copy in edges(STEPS - 1, c):
            copy.wait_send()
    for copy in early + exchange:
        copy.wait_send()


def write_back(value, inflow, value_out, inflow_out, sem):
    levels = value.shape[2] // 4
    copies = [pltpu.make_async_copy(inflow, inflow_out, sem.at[4])]
    for i in range(4):
        part = pl.ds(i * levels, levels)
        copies.append(pltpu.make_async_copy(value.at[:, :, part], value_out.at[:, :, part], sem.at[i]))
    for copy in copies:
        copy.start()
    for copy in copies:
        copy.wait()


def per_device(count, tracers, diffusivity, conductance, face_velocity, partner, weight, sea_mask):
    _, trac, lev, width, rows = tracers.shape
    chunks = lev // CHUNK
    full = (lev, width, rows)
    flat = (width, rows)
    anywhere = pl.BlockSpec(memory_space=pltpu.HBM)
    edge = (STEPS, chunks, trac, CHUNK, rows)
    dma = pltpu.SemaphoreType.DMA
    real = jnp.float32
    shapes = (
        jax.ShapeDtypeStruct(tracers.shape, real),
        jax.ShapeDtypeStruct((1, trac, width, rows), real),
    )
    vmem = pl.BlockSpec(memory_space=pltpu.VMEM)
    results = pl.pallas_call(
        functools.partial(kernel, count),
        out_shape=shapes,
        in_specs=[anywhere] * 7,
        out_specs=(vmem, vmem),
        scratch_shapes=[
            pltpu.VMEM((trac,) + full, real),
            pltpu.VMEM(full, real),
            pltpu.VMEM(full, real),
            pltpu.VMEM(full, real),
            pltpu.VMEM(full, real),
            pltpu.VMEM(full, real),
            pltpu.VMEM(full, real),
            pltpu.VMEM(full, real),
            pltpu.VMEM(edge, real),
            pltpu.VMEM(edge, real),
            pltpu.VMEM((lev, rows), real),
            pltpu.VMEM(flat, jnp.int32),
            pltpu.VMEM((width // 2, rows), jnp.int32),
            pltpu.VMEM((width // 2, rows), jnp.int32),
            pltpu.VMEM((trac + 2,) + flat, real),
            pltpu.VMEM((trac + 2, 3 * width, rows), real),
            pltpu.VMEM((2,) + flat, jnp.int32),
            pltpu.VMEM((2,) + flat, jnp.int32),
            dma((6,)),
            dma((chunks,)),
            dma((8,)),
            dma((8,)),
            dma((2, STEPS, chunks)),
            dma((2, STEPS, chunks)),
        ],
        compiler_params=pltpu.CompilerParams(
            collective_id=0, has_side_effects=True, vmem_limit_bytes=34 * 1024 * 1024
        ),
        name="coupled_step",
    )(*[pltpu.with_memory_space_constraint(a, pltpu.HBM) for a in (tracers, diffusivity, conductance, face_velocity, partner, weight, sea_mask)])
    return pl.pallas_call(
        write_back,
        out_shape=shapes,
        in_specs=[vmem, vmem],
        out_specs=(anywhere, anywhere),
        scratch_shapes=[dma((5,))],
        compiler_params=pltpu.CompilerParams(vmem_limit_bytes=1024 * 1024),
        name="write_back",
    )(*results)


def solution(mesh):
    in_specs = (
        P("mp", None, None, "tile", None),
        P("mp", None, "tile", None),
        P("mp", "tile", None),
        P("mp", None, "tile", None),
        P("mp", None, "tile", None),
        P("mp", None, "tile", None),
        P("tile", None),
    )
    out_specs = (P("mp", None, None, "tile", None), P("mp", None, "tile", None))
    return jax.shard_map(
        functools.partial(per_device, mesh.shape["tile"]),
        mesh=mesh,
        in_specs=in_specs,
        out_specs=out_specs,
        check_vma=False,
    )
```

```python
import functools

import jax
import jax.numpy as jnp
from jax import lax
from jax.experimental import pallas as pl
from jax.experimental.pallas import tpu as pltpu
from jax.sharding import PartitionSpec as P

STEPS = 4
QUANT = 16
CHUNK = 8
REACH = 9
EARLY = 4

diffusion_nu = 0.12
MESH = pl.DeviceIdType.MESH


def kernel(
    count,
    tracers,
    diffusivity,
    conductance,
    velocity,
    partner,
    weight,
    sea_mask,
    out,
    inflow_out,
    spare,
    lower,
    ratio,
    inverse,
    speed,
    keep,
    east,
    west,
    from_left,
    from_right,
    speed_left,
    mask_own,
    mask_left,
    mask_right,
    terms,
    wide,
    partner_own,
    weight_own,
    response,
    response_edge,
    inflow_edge,
    load_sem,
    tracer_sem,
    misc_send,
    misc_recv,
    edge_send,
    edge_recv,
    reply_send,
    reply_recv,
):
    _, trac, lev, width, rows = out.shape
    field = out.at[0]
    inflow = inflow_out.at[0]
    fields = (field, spare)
    chunks = lev // CHUNK
    component = lax.axis_index("mp")
    tile = lax.axis_index("tile")
    other = 1 - component
    right = lax.rem(tile + 1, count)
    left = lax.rem(tile + count - 1, count)
    half = width // 2

    def chunk_load(c):
        part = pl.ds(c * CHUNK, CHUNK)
        return pltpu.make_async_copy(tracers.at[0, :, part], field.at[:, part], tracer_sem.at[c])

    loads = [
        pltpu.make_async_copy(source, target, load_sem.at[i])
        for i, (source, target) in enumerate(
            [
                (diffusivity.at[0], lower.at[pl.ds(0, lev - 1)]),
                (conductance.at[0], terms.at[trac + 1]),
                (sea_mask, mask_own),
                (velocity.at[0], speed),
                (partner.at[0], partner_own),
                (weight.at[0], weight_own),
            ]
        )
    ]
    loads[0].start()
    for c in range(chunks):
        chunk_load(c).start()
    loads[1].start()

    barrier = pltpu.get_barrier_semaphore()
    peers = [(component, left), (component, right), (other, tile), (other, left), (other, right)]
    for peer in peers:
        pl.semaphore_signal(barrier, inc=1, device_id=peer, device_id_type=MESH)
    pl.semaphore_wait(barrier, len(peers))

    def send(index, source, target, peer):
        return pltpu.make_async_remote_copy(
            src_ref=source,
            dst_ref=target,
            send_sem=misc_send.at[index],
            recv_sem=misc_recv.at[index],
            device_id=peer,
            device_id_type=MESH,
        )

    early = [
        send(0, velocity.at[0, :, width - 1], speed_left, (component, right)),
        send(1, sea_mask.at[pl.ds(half, half)], mask_left, (component, right)),
        send(2, sea_mask.at[pl.ds(0, half)], mask_right, (component, left)),
    ]

    def exchange_of(base, begin, size):
        ch = pl.ds(begin, size)
        moves = [
            (pl.ds(0, width), pl.ds(width, width), tile),
            (pl.ds(half, half), pl.ds(half, half), right),
            (half - 1, half - 1, right),
            (pl.ds(0, half), pl.ds(2 * width, half), left),
            (half, 2 * width + half, left),
        ]
        return [
            send(base + i, terms.at[ch, mine], wide.at[ch, theirs], (other, peer))
            for i, (mine, theirs, peer) in enumerate(moves)
        ]

    exchange_late = exchange_of(3, 0, trac)
    exchange_early = exchange_of(8, trac, 2)
    exchange = exchange_late + exchange_early
    for copy in early:
        copy.start()

    def edges(s, c, source=None):
        part = pl.ds(c * CHUNK, CHUNK)
        source = fields[s % 2] if source is None else source
        return [
            pltpu.make_async_remote_copy(
                src_ref=source.at[:, part, column],
                dst_ref=target.at[s, c],
                send_sem=edge_send.at[side, s, c],
                recv_sem=edge_recv.at[side, s, c],
                device_id=(component, peer),
                device_id_type=MESH,
            )
            for side, (column, target, peer) in enumerate(
                [(width - 1, from_left, right), (0, from_right, left)]
            )
        ]

    sides = [(width - 1, right), (0, left)]

    def replies(i):
        return [
            pltpu.make_async_remote_copy(
                src_ref=response.at[i, :, column],
                dst_ref=response_edge.at[side, i],
                send_sem=reply_send.at[side, i],
                recv_sem=reply_recv.at[side, i],
                device_id=(component, peer),
                device_id_type=MESH,
            )
            for side, (column, peer) in enumerate(sides)
        ]

    inflow_sends = [
        send(13 + side, inflow.at[:, column], inflow_edge.at[side], (component, peer))
        for side, (column, peer) in enumerate(sides)
    ]

    loads[0].wait()
    zero = jnp.zeros((width, rows), jnp.float32)
    lower[lev - 1] = zero

    def factor(l, carry):
        low, ratio_prev = carry
        high = lower[l]
        inv = 1.0 / (1.0 + low + high - low * ratio_prev)
        ratio_now = high * inv
        inverse[l] = inv
        lower[l] = low * inv
        ratio[l] = ratio_now
        return high, ratio_now

    lax.fori_loop(0, lev, factor, (zero, zero))
    slope = inverse[lev - 1]
    ratio[lev - 1] = slope
    terms[trac] = slope
    loads[1].wait()
    for copy in exchange_early:
        copy.start()

    def down_chunk(c, carry):
        chunk_load(c).wait()

        def down(k, partial):
            l = c * CHUNK + k
            low = lower[l]
            inv = inverse[l]
            now = tuple(field[t, l] * inv + low * partial[t] for t in range(trac))
            for t in range(trac):
                field[t, l] = now[t]
            return now

        return lax.fori_loop(0, CHUNK, down, carry)

    finals = lax.fori_loop(0, chunks, down_chunk, (zero,) * trac)
    for t in range(trac):
        terms[t] = finals[t]
    for copy in exchange_late:
        copy.start()
    for load in loads[2:]:
        load.start()

    def early_chunk(i, carry):
        c = chunks - 1 - i

        def up(k, above):
            l = c * CHUNK + CHUNK - 1 - k
            slant = ratio[l]
            now = tuple(field[t, l] + slant * above[t] for t in range(trac))
            for t in range(trac):
                spare[t, l] = now[t]
            reply = slant * above[trac]
            response[i, CHUNK - 1 - k] = reply
            return now + (reply,)

        carry = lax.fori_loop(0, CHUNK, up, carry, unroll=True)
        for copy in edges(0, c, spare) + replies(i):
            copy.start()
        return carry

    lax.fori_loop(0, EARLY, early_chunk, (zero,) * trac + (jnp.ones((width, rows), jnp.float32),))

    for load in loads[2:]:
        load.wait()
    for copy in early:
        copy.wait_recv()
    row = lax.broadcasted_iota(jnp.int32, (width, rows), 0)
    lane = lax.broadcasted_iota(jnp.int32, (width, rows), 1)
    first = row == 0
    last = row == width - 1

    def openness_of(mask):
        return jnp.where(component == 1, mask.astype(jnp.float32), jnp.ones(mask.shape, jnp.float32))

    openness = openness_of(mask_own[...])
    open_right = openness_of(mask_right[pl.ds(0, 1), :])
    open_left = openness_of(mask_left[pl.ds(half - 1, 1), :])
    open_east = openness * jnp.where(last, open_right, pltpu.roll(openness, width - 1, 0))
    open_west = openness * jnp.where(first, open_left, pltpu.roll(openness, 1, 0))
    north = jnp.where(lane == rows - 1, 0.0, diffusion_nu * openness * pltpu.roll(openness, rows - 1, 1))
    south = jnp.where(lane == 0, 0.0, diffusion_nu * openness * pltpu.roll(openness, 1, 1))

    def coefficients(l, _):
        here = speed[l]
        before = jnp.where(first, speed_left[pl.ds(l, 1), :], pltpu.roll(here, 1, 0))
        keep[l] = (
            1.0
            - north
            - south
            - open_east * (jnp.maximum(here, 0.0) + diffusion_nu)
            + open_west * (jnp.minimum(before, 0.0) - diffusion_nu)
        )
        east[l] = open_east * (diffusion_nu - jnp.minimum(here, 0.0))
        west[l] = open_west * (jnp.maximum(before, 0.0) + diffusion_nu)
        return 0

    lax.fori_loop(0, lev, coefficients, 0)

    for copy in exchange:
        copy.wait_recv()
    columns = count * width
    lanes = 128

    def surface(j, _):
        part = pl.ds(pl.multiple_of(j * lanes, lanes), lanes)
        for h in range(2):
            own_rows = pl.ds(h * half, half)
            place = tile * width + h * half + lax.broadcasted_iota(jnp.int32, (half, lanes), 0)
            own = [terms[ch, own_rows, part] for ch in range(trac + 2)]
            total = [jnp.zeros((half, lanes), jnp.float32) for _ in range(trac)]
            distance = [
                lax.rem(partner_own[k, own_rows, part] - place + (REACH + columns), columns)
                for k in range(2)
            ]
            peer = [[jnp.zeros((half, lanes), jnp.float32)] * (trac + 2) for k in range(2)]
            for offset in range(2 * REACH + 1):
                begin = width - REACH + offset + h * half
                hit = [distance[k] == offset for k in range(2)]
                for ch in range(trac + 2):
                    window = wide[ch, pl.ds(begin, half), part]
                    for k in range(2):
                        peer[k][ch] = jnp.where(hit[k], window, peer[k][ch])
            for k in range(2):
                series = own[trac + 1] * peer[k][trac + 1] / (own[trac + 1] + peer[k][trac + 1])
                scale = (
                    weight_own[k, own_rows, part].astype(jnp.float32)
                    * series
                    / (1.0 + series * (own[trac] + peer[k][trac]))
                )
                for t in range(trac):
                    total[t] = total[t] + scale * (own[t] - peer[k][t])
            for t in range(trac):
                inflow[t, own_rows, part] = total[t] * (-1.0 / QUANT)
        return 0

    lax.fori_loop(0, rows // lanes, surface, 0)

    for copy in inflow_sends:
        copy.start()

    def up_chunk(i, carry):
        c = chunks - 1 - i

        def up(k, above):
            l = c * CHUNK + CHUNK - 1 - k
            slant = ratio[l]
            now = tuple(field[t, l] + slant * above[t] for t in range(trac))
            for t in range(trac):
                field[t, l] = now[t]
            return now

        carry = lax.fori_loop(0, CHUNK, up, carry)

        @pl.when(i >= EARLY)
        def _():
            for copy in edges(0, c):
                copy.start()

        return carry

    lax.fori_loop(0, chunks, up_chunk, tuple(inflow[t] for t in range(trac)))

    def step(s):
        source, target = fields[s % 2], fields[(s + 1) % 2]

        def unit(i, _):
            c = chunks - 1 - i
            if s == 1:

                @pl.when(i >= EARLY)
                def _():
                    for copy in edges(0, c):
                        copy.wait_send()

            if s > 1:
                for copy in edges(s - 1, c):
                    copy.wait_send()
            for copy in edges(s, c):
                copy.wait_recv()
            if s == 0:

                @pl.when(i == 0)
                def _():
                    for copy in inflow_sends:
                        copy.wait_recv()

                @pl.when(i < EARLY)
                def _():
                    for copy in edges(0, c, spare) + replies(i):
                        copy.wait_send()
                    for copy in replies(i):
                        copy.wait_recv()
                    for side, edge in enumerate((from_left, from_right)):
                        for t in range(trac):
                            edge[0, c, t] = edge[0, c, t] + response_edge[side, i] * inflow_edge[side, pl.ds(t, 1), :]


            def level(k, _):
                l = c * CHUNK + k
                keep_l = keep[l]
                east_l = east[l]
                west_l = west[l]
                for t in range(trac):
                    here = source[t, l]
                    after = jnp.where(last, from_right[s, c, t, pl.ds(k, 1), :], pltpu.roll(here, width - 1, 0))
                    before = jnp.where(first, from_left[s, c, t, pl.ds(k, 1), :], pltpu.roll(here, 1, 0))
                    target[t, l] = (
                        keep_l * here
                        + east_l * after
                        + west_l * before
                        + north * pltpu.roll(here, rows - 1, 1)
                        + south * pltpu.roll(here, 1, 1)
                    )
                return 0

            lax.fori_loop(0, CHUNK, level, 0, unroll=True)
            if s < STEPS - 1:
                for copy in edges(s + 1, c):
                    copy.start()
            return 0

        lax.fori_loop(0, chunks, unit, 0)

    for s in range(STEPS):
        step(s)

    for c in range(chunks):
        for copy in edges(STEPS - 1, c):
            copy.wait_send()
    for copy in early + exchange + inflow_sends:
        copy.wait_send()


def write_back(value, inflow, value_out, inflow_out, sem):
    levels = value.shape[2] // 4
    copies = [pltpu.make_async_copy(inflow, inflow_out, sem.at[4])]
    for i in range(4):
        part = pl.ds(i * levels, levels)
        copies.append(pltpu.make_async_copy(value.at[:, :, part], value_out.at[:, :, part], sem.at[i]))
    for copy in copies:
        copy.start()
    for copy in copies:
        copy.wait()


def per_device(count, tracers, diffusivity, conductance, face_velocity, partner, weight, sea_mask):
    _, trac, lev, width, rows = tracers.shape
    chunks = lev // CHUNK
    full = (lev, width, rows)
    flat = (width, rows)
    anywhere = pl.BlockSpec(memory_space=pltpu.HBM)
    edge = (STEPS, chunks, trac, CHUNK, rows)
    dma = pltpu.SemaphoreType.DMA
    real = jnp.float32
    shapes = (
        jax.ShapeDtypeStruct(tracers.shape, real),
        jax.ShapeDtypeStruct((1, trac, width, rows), real),
    )
    vmem = pl.BlockSpec(memory_space=pltpu.VMEM)
    results = pl.pallas_call(
        functools.partial(kernel, count),
        out_shape=shapes,
        in_specs=[anywhere] * 7,
        out_specs=(vmem, vmem),
        scratch_shapes=[
            pltpu.VMEM((trac,) + full, real),
            pltpu.VMEM(full, real),
            pltpu.VMEM(full, real),
            pltpu.VMEM(full, real),
            pltpu.VMEM(full, real),
            pltpu.VMEM(full, real),
            pltpu.VMEM(full, real),
            pltpu.VMEM(full, real),
            pltpu.VMEM(edge, real),
            pltpu.VMEM(edge, real),
            pltpu.VMEM((lev, rows), real),
            pltpu.VMEM(flat, jnp.int32),
            pltpu.VMEM((width // 2, rows), jnp.int32),
            pltpu.VMEM((width // 2, rows), jnp.int32),
            pltpu.VMEM((trac + 2,) + flat, real),
            pltpu.VMEM((trac + 2, 3 * width, rows), real),
            pltpu.VMEM((2,) + flat, jnp.int32),
            pltpu.VMEM((2,) + flat, jnp.int32),
            pltpu.VMEM((EARLY, CHUNK) + flat, real),
            pltpu.VMEM((2, EARLY, CHUNK, rows), real),
            pltpu.VMEM((2, trac, rows), real),
            dma((6,)),
            dma((chunks,)),
            dma((15,)),
            dma((15,)),
            dma((2, STEPS, chunks)),
            dma((2, STEPS, chunks)),
            dma((2, EARLY)),
            dma((2, EARLY)),
        ],
        compiler_params=pltpu.CompilerParams(
            collective_id=0, has_side_effects=True, vmem_limit_bytes=34 * 1024 * 1024
        ),
        name="coupled_step",
    )(*[pltpu.with_memory_space_constraint(a, pltpu.HBM) for a in (tracers, diffusivity, conductance, face_velocity, partner, weight, sea_mask)])
    return pl.pallas_call(
        write_back,
        out_shape=shapes,
        in_specs=[vmem, vmem],
        out_specs=(anywhere, anywhere),
        scratch_shapes=[dma((5,))],
        compiler_params=pltpu.CompilerParams(vmem_limit_bytes=1024 * 1024),
        name="write_back",
    )(*results)


def solution(mesh):
    in_specs = (
        P("mp", None, None, "tile", None),
        P("mp", None, "tile", None),
        P("mp", "tile", None),
        P("mp", None, "tile", None),
        P("mp", None, "tile", None),
        P("mp", None, "tile", None),
        P("tile", None),
    )
    out_specs = (P("mp", None, None, "tile", None), P("mp", None, "tile", None))
    return jax.shard_map(
        functools.partial(per_device, mesh.shape["tile"]),
        mesh=mesh,
        in_specs=in_specs,
        out_specs=out_specs,
        check_vma=False,
    )
```

```python
import functools

import jax
import jax.numpy as jnp
from jax import lax
from jax.experimental import pallas as pl
from jax.experimental.pallas import tpu as pltpu
from jax.sharding import PartitionSpec as P

STEPS = 4
QUANT = 16
CHUNK = 8
REACH = 9
EARLY = 4

diffusion_nu = 0.12
MESH = pl.DeviceIdType.MESH


def kernel(
    count,
    tracers,
    diffusivity,
    conductance,
    velocity,
    partner,
    weight,
    sea_mask,
    out,
    inflow_out,
    spare,
    lower,
    ratio,
    inverse,
    speed,
    keep,
    east,
    west,
    from_left,
    from_right,
    speed_left,
    mask_own,
    mask_left,
    mask_right,
    terms,
    wide,
    partner_own,
    weight_own,
    response,
    response_edge,
    inflow_edge,
    load_sem,
    tracer_sem,
    misc_send,
    misc_recv,
    edge_send,
    edge_recv,
    reply_send,
    reply_recv,
):
    _, trac, lev, width, rows = out.shape
    field = out.at[0]
    inflow = inflow_out.at[0]
    fields = (field, spare)
    chunks = lev // CHUNK
    component = lax.axis_index("mp")
    tile = lax.axis_index("tile")
    other = 1 - component
    right = lax.rem(tile + 1, count)
    left = lax.rem(tile + count - 1, count)
    half = width // 2

    def chunk_load(c):
        part = pl.ds(c * CHUNK, CHUNK)
        return pltpu.make_async_copy(tracers.at[0, :, part], field.at[:, part], tracer_sem.at[c])

    loads = [
        pltpu.make_async_copy(source, target, load_sem.at[i])
        for i, (source, target) in enumerate(
            [
                (diffusivity.at[0], lower.at[pl.ds(0, lev - 1)]),
                (conductance.at[0], terms.at[trac + 1]),
                (sea_mask, mask_own),
                (velocity.at[0], speed),
                (partner.at[0], partner_own),
                (weight.at[0], weight_own),
            ]
        )
    ]
    loads[0].start()
    for c in range(chunks):
        chunk_load(c).start()
    for load in loads[1:]:
        load.start()

    barrier = pltpu.get_barrier_semaphore()
    peers = [(component, left), (component, right), (other, tile), (other, left), (other, right)]
    for peer in peers:
        pl.semaphore_signal(barrier, inc=1, device_id=peer, device_id_type=MESH)
    pl.semaphore_wait(barrier, len(peers))

    def send(index, source, target, peer):
        return pltpu.make_async_remote_copy(
            src_ref=source,
            dst_ref=target,
            send_sem=misc_send.at[index],
            recv_sem=misc_recv.at[index],
            device_id=peer,
            device_id_type=MESH,
        )

    early = [
        send(0, velocity.at[0, :, width - 1], speed_left, (component, right)),
        send(1, sea_mask.at[pl.ds(half, half)], mask_left, (component, right)),
        send(2, sea_mask.at[pl.ds(0, half)], mask_right, (component, left)),
    ]

    def exchange_of(base, begin, size):
        ch = pl.ds(begin, size)
        moves = [
            (pl.ds(0, width), pl.ds(width, width), tile),
            (pl.ds(half, half), pl.ds(half, half), right),
            (half - 1, half - 1, right),
            (pl.ds(0, half), pl.ds(2 * width, half), left),
            (half, 2 * width + half, left),
        ]
        return [
            send(base + i, terms.at[ch, mine], wide.at[ch, theirs], (other, peer))
            for i, (mine, theirs, peer) in enumerate(moves)
        ]

    exchange_late = exchange_of(3, 0, trac)
    exchange_early = exchange_of(8, trac, 2)
    exchange = exchange_late + exchange_early
    for copy in early:
        copy.start()

    def edges(s, c, source=None):
        part = pl.ds(c * CHUNK, CHUNK)
        source = fields[s % 2] if source is None else source
        return [
            pltpu.make_async_remote_copy(
                src_ref=source.at[:, part, column],
                dst_ref=target.at[s, c],
                send_sem=edge_send.at[side, s, c],
                recv_sem=edge_recv.at[side, s, c],
                device_id=(component, peer),
                device_id_type=MESH,
            )
            for side, (column, target, peer) in enumerate(
                [(width - 1, from_left, right), (0, from_right, left)]
            )
        ]

    sides = [(width - 1, right), (0, left)]

    def replies(i):
        return [
            pltpu.make_async_remote_copy(
                src_ref=response.at[i, :, column],
                dst_ref=response_edge.at[side, i],
                send_sem=reply_send.at[side, i],
                recv_sem=reply_recv.at[side, i],
                device_id=(component, peer),
                device_id_type=MESH,
            )
            for side, (column, peer) in enumerate(sides)
        ]

    inflow_sends = [
        send(13 + side, inflow.at[:, column], inflow_edge.at[side], (component, peer))
        for side, (column, peer) in enumerate(sides)
    ]

    loads[0].wait()
    zero = jnp.zeros((width, rows), jnp.float32)
    lower[lev - 1] = zero

    def factor(l, carry):
        low, ratio_prev = carry
        high = lower[l]
        inv = 1.0 / (1.0 + low + high - low * ratio_prev)
        ratio_now = high * inv
        inverse[l] = inv
        lower[l] = low * inv
        ratio[l] = ratio_now
        return high, ratio_now

    lax.fori_loop(0, lev, factor, (zero, zero), unroll=4)
    slope = inverse[lev - 1]
    ratio[lev - 1] = slope
    terms[trac] = slope
    loads[1].wait()
    for copy in exchange_early:
        copy.start()

    def down_chunk(c, carry):
        chunk_load(c).wait()

        def down(k, partial):
            l = c * CHUNK + k
            low = lower[l]
            inv = inverse[l]
            now = tuple(field[t, l] * inv + low * partial[t] for t in range(trac))
            for t in range(trac):
                field[t, l] = now[t]
            return now

        return lax.fori_loop(0, CHUNK, down, carry, unroll=4)

    finals = lax.fori_loop(0, chunks, down_chunk, (zero,) * trac)
    for t in range(trac):
        terms[t] = finals[t]
    for copy in exchange_late:
        copy.start()

    def early_chunk(i, carry):
        c = chunks - 1 - i

        def up(k, above):
            l = c * CHUNK + CHUNK - 1 - k
            slant = ratio[l]
            now = tuple(field[t, l] + slant * above[t] for t in range(trac))
            for t in range(trac):
                spare[t, l] = now[t]
            reply = slant * above[trac]
            response[i, CHUNK - 1 - k] = reply
            return now + (reply,)

        carry = lax.fori_loop(0, CHUNK, up, carry, unroll=True)
        for copy in edges(0, c, spare) + replies(i):
            copy.start()
        return carry

    lax.fori_loop(0, EARLY, early_chunk, (zero,) * trac + (jnp.ones((width, rows), jnp.float32),))

    for load in loads[2:]:
        load.wait()
    for copy in early:
        copy.wait_recv()
    row = lax.broadcasted_iota(jnp.int32, (width, rows), 0)
    lane = lax.broadcasted_iota(jnp.int32, (width, rows), 1)
    first = row == 0
    last = row == width - 1

    def openness_of(mask):
        return jnp.where(component == 1, mask.astype(jnp.float32), jnp.ones(mask.shape, jnp.float32))

    openness = openness_of(mask_own[...])
    open_right = openness_of(mask_right[pl.ds(0, 1), :])
    open_left = openness_of(mask_left[pl.ds(half - 1, 1), :])
    open_east = openness * jnp.where(last, open_right, pltpu.roll(openness, width - 1, 0))
    open_west = openness * jnp.where(first, open_left, pltpu.roll(openness, 1, 0))
    north = jnp.where(lane == rows - 1, 0.0, diffusion_nu * openness * pltpu.roll(openness, rows - 1, 1))
    south = jnp.where(lane == 0, 0.0, diffusion_nu * openness * pltpu.roll(openness, 1, 1))

    def coefficients(l, _):
        here = speed[l]
        before = jnp.where(first, speed_left[pl.ds(l, 1), :], pltpu.roll(here, 1, 0))
        keep[l] = (
            1.0
            - north
            - south
            - open_east * (jnp.maximum(here, 0.0) + diffusion_nu)
            + open_west * (jnp.minimum(before, 0.0) - diffusion_nu)
        )
        east[l] = open_east * (diffusion_nu - jnp.minimum(here, 0.0))
        west[l] = open_west * (jnp.maximum(before, 0.0) + diffusion_nu)
        return 0

    lax.fori_loop(0, lev, coefficients, 0)

    for copy in exchange:
        copy.wait_recv()
    columns = count * width
    lanes = 128

    def surface(j, _):
        part = pl.ds(pl.multiple_of(j * lanes, lanes), lanes)
        for h in range(2):
            own_rows = pl.ds(h * half, half)
            place = tile * width + h * half + lax.broadcasted_iota(jnp.int32, (half, lanes), 0)
            own = [terms[ch, own_rows, part] for ch in range(trac + 2)]
            total = [jnp.zeros((half, lanes), jnp.float32) for _ in range(trac)]
            distance = [
                lax.rem(partner_own[k, own_rows, part] - place + (REACH + columns), columns)
                for k in range(2)
            ]
            peer = [[jnp.zeros((half, lanes), jnp.float32)] * (trac + 2) for k in range(2)]
            for offset in range(2 * REACH + 1):
                begin = width - REACH + offset + h * half
                hit = [distance[k] == offset for k in range(2)]
                for ch in range(trac + 2):
                    window = wide[ch, pl.ds(begin, half), part]
                    for k in range(2):
                        peer[k][ch] = jnp.where(hit[k], window, peer[k][ch])
            for k in range(2):
                series = own[trac + 1] * peer[k][trac + 1] / (own[trac + 1] + peer[k][trac + 1])
                scale = (
                    weight_own[k, own_rows, part].astype(jnp.float32)
                    * series
                    / (1.0 + series * (own[trac] + peer[k][trac]))
                )
                for t in range(trac):
                    total[t] = total[t] + scale * (own[t] - peer[k][t])
            for t in range(trac):
                inflow[t, own_rows, part] = total[t] * (-1.0 / QUANT)
        return 0

    lax.fori_loop(0, rows // lanes, surface, 0)

    for copy in inflow_sends:
        copy.start()

    def up_chunk(i, carry):
        c = chunks - 1 - i

        def up(k, above):
            l = c * CHUNK + CHUNK - 1 - k
            slant = ratio[l]
            now = tuple(field[t, l] + slant * above[t] for t in range(trac))
            for t in range(trac):
                field[t, l] = now[t]
            return now

        carry = lax.fori_loop(0, CHUNK, up, carry)

        @pl.when(i >= EARLY)
        def _():
            for copy in edges(0, c):
                copy.start()

        return carry

    lax.fori_loop(0, chunks, up_chunk, tuple(inflow[t] for t in range(trac)))

    def step(s):
        source, target = fields[s % 2], fields[(s + 1) % 2]

        def unit(i, _):
            c = chunks - 1 - i
            if s == 1:

                @pl.when(i >= EARLY)
                def _():
                    for copy in edges(0, c):
                        copy.wait_send()

            if s > 1:
                for copy in edges(s - 1, c):
                    copy.wait_send()
            for copy in edges(s, c):
                copy.wait_recv()
            if s == 0:

                @pl.when(i == 0)
                def _():
                    for copy in inflow_sends:
                        copy.wait_recv()

                @pl.when(i < EARLY)
                def _():
                    for copy in edges(0, c, spare) + replies(i):
                        copy.wait_send()
                    for copy in replies(i):
                        copy.wait_recv()
                    for side, edge in enumerate((from_left, from_right)):
                        for t in range(trac):
                            edge[0, c, t] = edge[0, c, t] + response_edge[side, i] * inflow_edge[side, pl.ds(t, 1), :]


            def level(k, _):
                l = c * CHUNK + k
                keep_l = keep[l]
                east_l = east[l]
                west_l = west[l]
                for t in range(trac):
                    here = source[t, l]
                    after = jnp.where(last, from_right[s, c, t, pl.ds(k, 1), :], pltpu.roll(here, width - 1, 0))
                    before = jnp.where(first, from_left[s, c, t, pl.ds(k, 1), :], pltpu.roll(here, 1, 0))
                    target[t, l] = (
                        keep_l * here
                        + east_l * after
                        + west_l * before
                        + north * pltpu.roll(here, rows - 1, 1)
                        + south * pltpu.roll(here, 1, 1)
                    )
                return 0

            lax.fori_loop(0, CHUNK, level, 0, unroll=True)
            if s < STEPS - 1:
                for copy in edges(s + 1, c):
                    copy.start()
            return 0

        lax.fori_loop(0, chunks, unit, 0)

    for s in range(STEPS):
        step(s)

    for c in range(chunks):
        for copy in edges(STEPS - 1, c):
            copy.wait_send()
    for copy in early + exchange + inflow_sends:
        copy.wait_send()


def write_back(value, inflow, value_out, inflow_out, sem):
    levels = value.shape[2] // 4
    copies = [pltpu.make_async_copy(inflow, inflow_out, sem.at[4])]
    for i in range(4):
        part = pl.ds(i * levels, levels)
        copies.append(pltpu.make_async_copy(value.at[:, :, part], value_out.at[:, :, part], sem.at[i]))
    for copy in copies:
        copy.start()
    for copy in copies:
        copy.wait()


def per_device(count, tracers, diffusivity, conductance, face_velocity, partner, weight, sea_mask):
    _, trac, lev, width, rows = tracers.shape
    chunks = lev // CHUNK
    full = (lev, width, rows)
    flat = (width, rows)
    anywhere = pl.BlockSpec(memory_space=pltpu.HBM)
    edge = (STEPS, chunks, trac, CHUNK, rows)
    dma = pltpu.SemaphoreType.DMA
    real = jnp.float32
    shapes = (
        jax.ShapeDtypeStruct(tracers.shape, real),
        jax.ShapeDtypeStruct((1, trac, width, rows), real),
    )
    vmem = pl.BlockSpec(memory_space=pltpu.VMEM)
    results = pl.pallas_call(
        functools.partial(kernel, count),
        out_shape=shapes,
        in_specs=[anywhere] * 7,
        out_specs=(vmem, vmem),
        scratch_shapes=[
            pltpu.VMEM((trac,) + full, real),
            pltpu.VMEM(full, real),
            pltpu.VMEM(full, real),
            pltpu.VMEM(full, real),
            pltpu.VMEM(full, real),
            pltpu.VMEM(full, real),
            pltpu.VMEM(full, real),
            pltpu.VMEM(full, real),
            pltpu.VMEM(edge, real),
            pltpu.VMEM(edge, real),
            pltpu.VMEM((lev, rows), real),
            pltpu.VMEM(flat, jnp.int32),
            pltpu.VMEM((width // 2, rows), jnp.int32),
            pltpu.VMEM((width // 2, rows), jnp.int32),
            pltpu.VMEM((trac + 2,) + flat, real),
            pltpu.VMEM((trac + 2, 3 * width, rows), real),
            pltpu.VMEM((2,) + flat, jnp.int32),
            pltpu.VMEM((2,) + flat, jnp.int32),
            pltpu.VMEM((EARLY, CHUNK) + flat, real),
            pltpu.VMEM((2, EARLY, CHUNK, rows), real),
            pltpu.VMEM((2, trac, rows), real),
            dma((6,)),
            dma((chunks,)),
            dma((15,)),
            dma((15,)),
            dma((2, STEPS, chunks)),
            dma((2, STEPS, chunks)),
            dma((2, EARLY)),
            dma((2, EARLY)),
        ],
        compiler_params=pltpu.CompilerParams(
            collective_id=0, has_side_effects=True, vmem_limit_bytes=34 * 1024 * 1024
        ),
        name="coupled_step",
    )(*[pltpu.with_memory_space_constraint(a, pltpu.HBM) for a in (tracers, diffusivity, conductance, face_velocity, partner, weight, sea_mask)])
    return pl.pallas_call(
        write_back,
        out_shape=shapes,
        in_specs=[vmem, vmem],
        out_specs=(anywhere, anywhere),
        scratch_shapes=[dma((5,))],
        compiler_params=pltpu.CompilerParams(vmem_limit_bytes=1024 * 1024),
        name="write_back",
    )(*results)


def solution(mesh):
    in_specs = (
        P("mp", None, None, "tile", None),
        P("mp", None, "tile", None),
        P("mp", "tile", None),
        P("mp", None, "tile", None),
        P("mp", None, "tile", None),
        P("mp", None, "tile", None),
        P("tile", None),
    )
    out_specs = (P("mp", None, None, "tile", None), P("mp", None, "tile", None))
    return jax.shard_map(
        functools.partial(per_device, mesh.shape["tile"]),
        mesh=mesh,
        in_specs=in_specs,
        out_specs=out_specs,
        check_vma=False,
    )
```

```python
import functools

import jax
import jax.numpy as jnp
from jax import lax
from jax.experimental import pallas as pl
from jax.experimental.pallas import tpu as pltpu
from jax.sharding import PartitionSpec as P

STEPS = 4
QUANT = 16
CHUNK = 8
REACH = 9
EARLY = 4

diffusion_nu = 0.12
MESH = pl.DeviceIdType.MESH


def kernel(
    count,
    tracers,
    diffusivity,
    conductance,
    velocity,
    partner,
    weight,
    sea_mask,
    out,
    inflow_out,
    spare,
    lower,
    ratio,
    inverse,
    speed,
    keep,
    east,
    west,
    from_left,
    from_right,
    speed_left,
    mask_own,
    mask_left,
    mask_right,
    terms,
    wide,
    partner_own,
    weight_own,
    response,
    response_edge,
    inflow_edge,
    load_sem,
    tracer_sem,
    misc_send,
    misc_recv,
    edge_send,
    edge_recv,
    reply_send,
    reply_recv,
):
    _, trac, lev, width, rows = out.shape
    field = out.at[0]
    inflow = inflow_out.at[0]
    fields = (field, spare)
    chunks = lev // CHUNK
    component = lax.axis_index("mp")
    tile = lax.axis_index("tile")
    other = 1 - component
    right = lax.rem(tile + 1, count)
    left = lax.rem(tile + count - 1, count)
    half = width // 2

    def chunk_load(c):
        part = pl.ds(c * CHUNK, CHUNK)
        return pltpu.make_async_copy(tracers.at[0, :, part], field.at[:, part], tracer_sem.at[c])

    loads = [
        pltpu.make_async_copy(source, target, load_sem.at[i])
        for i, (source, target) in enumerate(
            [
                (diffusivity.at[0], lower.at[pl.ds(0, lev - 1)]),
                (conductance.at[0], terms.at[trac + 1]),
                (sea_mask, mask_own),
                (velocity.at[0], speed),
                (partner.at[0], partner_own),
                (weight.at[0], weight_own),
            ]
        )
    ]
    loads[0].start()
    for c in range(chunks):
        chunk_load(c).start()
    for load in loads[1:]:
        load.start()

    barrier = pltpu.get_barrier_semaphore()
    peers = [(component, left), (component, right), (other, tile), (other, left), (other, right)]
    for peer in peers:
        pl.semaphore_signal(barrier, inc=1, device_id=peer, device_id_type=MESH)
    pl.semaphore_wait(barrier, len(peers))

    def send(index, source, target, peer):
        return pltpu.make_async_remote_copy(
            src_ref=source,
            dst_ref=target,
            send_sem=misc_send.at[index],
            recv_sem=misc_recv.at[index],
            device_id=peer,
            device_id_type=MESH,
        )

    early = [
        send(0, velocity.at[0, :, width - 1], speed_left, (component, right)),
        send(1, sea_mask.at[pl.ds(half, half)], mask_left, (component, right)),
        send(2, sea_mask.at[pl.ds(0, half)], mask_right, (component, left)),
    ]

    def exchange_of(base, begin, size):
        ch = pl.ds(begin, size)
        moves = [
            (pl.ds(0, width), pl.ds(width, width), tile),
            (pl.ds(half, half), pl.ds(half, half), right),
            (half - 1, half - 1, right),
            (pl.ds(0, half), pl.ds(2 * width, half), left),
            (half, 2 * width + half, left),
        ]
        return [
            send(base + i, terms.at[ch, mine], wide.at[ch, theirs], (other, peer))
            for i, (mine, theirs, peer) in enumerate(moves)
        ]

    exchange_late = exchange_of(3, 0, trac)
    exchange_early = exchange_of(8, trac, 2)
    exchange = exchange_late + exchange_early
    for copy in early:
        copy.start()

    def edges(s, c, source=None):
        part = pl.ds(c * CHUNK, CHUNK)
        source = fields[s % 2] if source is None else source
        return [
            pltpu.make_async_remote_copy(
                src_ref=source.at[:, part, column],
                dst_ref=target.at[s, c],
                send_sem=edge_send.at[side, s, c],
                recv_sem=edge_recv.at[side, s, c],
                device_id=(component, peer),
                device_id_type=MESH,
            )
            for side, (column, target, peer) in enumerate(
                [(width - 1, from_left, right), (0, from_right, left)]
            )
        ]

    sides = [(width - 1, right), (0, left)]

    def replies(i):
        return [
            pltpu.make_async_remote_copy(
                src_ref=response.at[i, :, column],
                dst_ref=response_edge.at[side, i],
                send_sem=reply_send.at[side, i],
                recv_sem=reply_recv.at[side, i],
                device_id=(component, peer),
                device_id_type=MESH,
            )
            for side, (column, peer) in enumerate(sides)
        ]

    inflow_sends = [
        send(13 + side, inflow.at[:, column], inflow_edge.at[side], (component, peer))
        for side, (column, peer) in enumerate(sides)
    ]

    loads[0].wait()
    zero = jnp.zeros((width, rows), jnp.float32)
    lower[lev - 1] = zero

    def factor(l, carry):
        low, ratio_prev = carry
        high = lower[l]
        inv = 1.0 / (1.0 + low + high - low * ratio_prev)
        ratio_now = high * inv
        inverse[l] = inv
        lower[l] = low * inv
        ratio[l] = ratio_now
        return high, ratio_now

    lax.fori_loop(0, lev, factor, (zero, zero), unroll=4)
    slope = inverse[lev - 1]
    ratio[lev - 1] = slope
    terms[trac] = slope
    loads[1].wait()
    for copy in exchange_early:
        copy.start()

    def down_chunk(c, carry):
        chunk_load(c).wait()

        def down(k, partial):
            l = c * CHUNK + k
            low = lower[l]
            inv = inverse[l]
            now = tuple(field[t, l] * inv + low * partial[t] for t in range(trac))
            for t in range(trac):
                field[t, l] = now[t]
            return now

        return lax.fori_loop(0, CHUNK, down, carry, unroll=4)

    finals = lax.fori_loop(0, chunks, down_chunk, (zero,) * trac)
    for t in range(trac):
        terms[t] = finals[t]
    for copy in exchange_late:
        copy.start()

    def early_chunk(i, carry):
        c = chunks - 1 - i

        def up(k, above):
            l = c * CHUNK + CHUNK - 1 - k
            slant = ratio[l]
            now = tuple(field[t, l] + slant * above[t] for t in range(trac))
            for t in range(trac):
                spare[t, l] = now[t]
            reply = slant * above[trac]
            response[i, CHUNK - 1 - k] = reply
            return now + (reply,)

        carry = lax.fori_loop(0, CHUNK, up, carry, unroll=True)
        for copy in edges(0, c, spare) + replies(i):
            copy.start()
        return carry

    lax.fori_loop(0, EARLY, early_chunk, (zero,) * trac + (jnp.ones((width, rows), jnp.float32),))

    for load in loads[2:]:
        load.wait()
    for copy in early:
        copy.wait_recv()
    row = lax.broadcasted_iota(jnp.int32, (width, rows), 0)
    lane = lax.broadcasted_iota(jnp.int32, (width, rows), 1)
    first = row == 0
    last = row == width - 1

    def openness_of(mask):
        return jnp.where(component == 1, mask.astype(jnp.float32), jnp.ones(mask.shape, jnp.float32))

    openness = openness_of(mask_own[...])
    open_right = openness_of(mask_right[pl.ds(0, 1), :])
    open_left = openness_of(mask_left[pl.ds(half - 1, 1), :])
    open_east = openness * jnp.where(last, open_right, pltpu.roll(openness, width - 1, 0))
    open_west = openness * jnp.where(first, open_left, pltpu.roll(openness, 1, 0))
    north = jnp.where(lane == rows - 1, 0.0, diffusion_nu * openness * pltpu.roll(openness, rows - 1, 1))
    south = jnp.where(lane == 0, 0.0, diffusion_nu * openness * pltpu.roll(openness, 1, 1))

    def coefficients(l, _):
        here = speed[l]
        before = jnp.where(first, speed_left[pl.ds(l, 1), :], pltpu.roll(here, 1, 0))
        keep[l] = (
            1.0
            - north
            - south
            - open_east * (jnp.maximum(here, 0.0) + diffusion_nu)
            + open_west * (jnp.minimum(before, 0.0) - diffusion_nu)
        )
        east[l] = open_east * (diffusion_nu - jnp.minimum(here, 0.0))
        west[l] = open_west * (jnp.maximum(before, 0.0) + diffusion_nu)
        return 0

    lax.fori_loop(0, lev, coefficients, 0, unroll=2)

    for copy in exchange:
        copy.wait_recv()
    columns = count * width
    lanes = 128

    def surface(j, _):
        part = pl.ds(pl.multiple_of(j * lanes, lanes), lanes)
        for h in range(2):
            own_rows = pl.ds(h * half, half)
            place = tile * width + h * half + lax.broadcasted_iota(jnp.int32, (half, lanes), 0)
            own = [terms[ch, own_rows, part] for ch in range(trac + 2)]
            total = [jnp.zeros((half, lanes), jnp.float32) for _ in range(trac)]
            distance = [
                lax.rem(partner_own[k, own_rows, part] - place + (REACH + columns), columns)
                for k in range(2)
            ]
            peer = [[jnp.zeros((half, lanes), jnp.float32)] * (trac + 2) for k in range(2)]
            for offset in range(2 * REACH + 1):
                begin = width - REACH + offset + h * half
                hit = [distance[k] == offset for k in range(2)]
                for ch in range(trac + 2):
                    window = wide[ch, pl.ds(begin, half), part]
                    for k in range(2):
                        peer[k][ch] = jnp.where(hit[k], window, peer[k][ch])
            for k in range(2):
                series = own[trac + 1] * peer[k][trac + 1] / (own[trac + 1] + peer[k][trac + 1])
                scale = (
                    weight_own[k, own_rows, part].astype(jnp.float32)
                    * series
                    / (1.0 + series * (own[trac] + peer[k][trac]))
                )
                for t in range(trac):
                    total[t] = total[t] + scale * (own[t] - peer[k][t])
            for t in range(trac):
                inflow[t, own_rows, part] = total[t] * (-1.0 / QUANT)
        return 0

    lax.fori_loop(0, rows // lanes, surface, 0)

    for copy in inflow_sends:
        copy.start()

    def up_chunk(i, carry):
        c = chunks - 1 - i

        def up(k, above):
            l = c * CHUNK + CHUNK - 1 - k
            slant = ratio[l]
            now = tuple(field[t, l] + slant * above[t] for t in range(trac))
            for t in range(trac):
                field[t, l] = now[t]
            return now

        carry = lax.fori_loop(0, CHUNK, up, carry, unroll=True)

        @pl.when(i >= EARLY)
        def _():
            for copy in edges(0, c):
                copy.start()

        return carry

    lax.fori_loop(0, chunks, up_chunk, tuple(inflow[t] for t in range(trac)))

    def step(s):
        source, target = fields[s % 2], fields[(s + 1) % 2]

        def unit(i, _):
            c = chunks - 1 - i
            if s == 1:

                @pl.when(i >= EARLY)
                def _():
                    for copy in edges(0, c):
                        copy.wait_send()

            if s > 1:
                for copy in edges(s - 1, c):
                    copy.wait_send()
            for copy in edges(s, c):
                copy.wait_recv()
            if s == 0:

                @pl.when(i == 0)
                def _():
                    for copy in inflow_sends:
                        copy.wait_recv()

                @pl.when(i < EARLY)
                def _():
                    for copy in edges(0, c, spare) + replies(i):
                        copy.wait_send()
                    for copy in replies(i):
                        copy.wait_recv()
                    for side, edge in enumerate((from_left, from_right)):
                        for t in range(trac):
                            edge[0, c, t] = edge[0, c, t] + response_edge[side, i] * inflow_edge[side, pl.ds(t, 1), :]


            def level(k, _):
                l = c * CHUNK + k
                keep_l = keep[l]
                east_l = east[l]
                west_l = west[l]
                for t in range(trac):
                    here = source[t, l]
                    after = jnp.where(last, from_right[s, c, t, pl.ds(k, 1), :], pltpu.roll(here, width - 1, 0))
                    before = jnp.where(first, from_left[s, c, t, pl.ds(k, 1), :], pltpu.roll(here, 1, 0))
                    target[t, l] = (
                        keep_l * here
                        + east_l * after
                        + west_l * before
                        + north * pltpu.roll(here, rows - 1, 1)
                        + south * pltpu.roll(here, 1, 1)
                    )
                return 0

            lax.fori_loop(0, CHUNK, level, 0, unroll=True)
            if s < STEPS - 1:
                for copy in edges(s + 1, c):
                    copy.start()
            return 0

        lax.fori_loop(0, chunks, unit, 0)

    for s in range(STEPS):
        step(s)

    for c in range(chunks):
        for copy in edges(STEPS - 1, c):
            copy.wait_send()
    for copy in early + exchange + inflow_sends:
        copy.wait_send()


def write_back(value, inflow, value_out, inflow_out, sem):
    levels = value.shape[2] // 4
    copies = [pltpu.make_async_copy(inflow, inflow_out, sem.at[4])]
    for i in range(4):
        part = pl.ds(i * levels, levels)
        copies.append(pltpu.make_async_copy(value.at[:, :, part], value_out.at[:, :, part], sem.at[i]))
    for copy in copies:
        copy.start()
    for copy in copies:
        copy.wait()


def per_device(count, tracers, diffusivity, conductance, face_velocity, partner, weight, sea_mask):
    _, trac, lev, width, rows = tracers.shape
    chunks = lev // CHUNK
    full = (lev, width, rows)
    flat = (width, rows)
    anywhere = pl.BlockSpec(memory_space=pltpu.HBM)
    edge = (STEPS, chunks, trac, CHUNK, rows)
    dma = pltpu.SemaphoreType.DMA
    real = jnp.float32
    shapes = (
        jax.ShapeDtypeStruct(tracers.shape, real),
        jax.ShapeDtypeStruct((1, trac, width, rows), real),
    )
    vmem = pl.BlockSpec(memory_space=pltpu.VMEM)
    results = pl.pallas_call(
        functools.partial(kernel, count),
        out_shape=shapes,
        in_specs=[anywhere] * 7,
        out_specs=(vmem, vmem),
        scratch_shapes=[
            pltpu.VMEM((trac,) + full, real),
            pltpu.VMEM(full, real),
            pltpu.VMEM(full, real),
            pltpu.VMEM(full, real),
            pltpu.VMEM(full, real),
            pltpu.VMEM(full, real),
            pltpu.VMEM(full, real),
            pltpu.VMEM(full, real),
            pltpu.VMEM(edge, real),
            pltpu.VMEM(edge, real),
            pltpu.VMEM((lev, rows), real),
            pltpu.VMEM(flat, jnp.int32),
            pltpu.VMEM((width // 2, rows), jnp.int32),
            pltpu.VMEM((width // 2, rows), jnp.int32),
            pltpu.VMEM((trac + 2,) + flat, real),
            pltpu.VMEM((trac + 2, 3 * width, rows), real),
            pltpu.VMEM((2,) + flat, jnp.int32),
            pltpu.VMEM((2,) + flat, jnp.int32),
            pltpu.VMEM((EARLY, CHUNK) + flat, real),
            pltpu.VMEM((2, EARLY, CHUNK, rows), real),
            pltpu.VMEM((2, trac, rows), real),
            dma((6,)),
            dma((chunks,)),
            dma((15,)),
            dma((15,)),
            dma((2, STEPS, chunks)),
            dma((2, STEPS, chunks)),
            dma((2, EARLY)),
            dma((2, EARLY)),
        ],
        compiler_params=pltpu.CompilerParams(
            collective_id=0, has_side_effects=True, vmem_limit_bytes=34 * 1024 * 1024
        ),
        name="coupled_step",
    )(*[pltpu.with_memory_space_constraint(a, pltpu.HBM) for a in (tracers, diffusivity, conductance, face_velocity, partner, weight, sea_mask)])
    return pl.pallas_call(
        write_back,
        out_shape=shapes,
        in_specs=[vmem, vmem],
        out_specs=(anywhere, anywhere),
        scratch_shapes=[dma((5,))],
        compiler_params=pltpu.CompilerParams(vmem_limit_bytes=1024 * 1024),
        name="write_back",
    )(*results)


def solution(mesh):
    in_specs = (
        P("mp", None, None, "tile", None),
        P("mp", None, "tile", None),
        P("mp", "tile", None),
        P("mp", None, "tile", None),
        P("mp", None, "tile", None),
        P("mp", None, "tile", None),
        P("tile", None),
    )
    out_specs = (P("mp", None, None, "tile", None), P("mp", None, "tile", None))
    return jax.shard_map(
        functools.partial(per_device, mesh.shape["tile"]),
        mesh=mesh,
        in_specs=in_specs,
        out_specs=out_specs,
        check_vma=False,
    )
```

```python
import functools

import jax
import jax.numpy as jnp
from jax import lax
from jax.experimental import pallas as pl
from jax.experimental.pallas import tpu as pltpu
from jax.sharding import PartitionSpec as P

STEPS = 4
QUANT = 16
CHUNK = 8
REACH = 9
EARLY = 4

diffusion_nu = 0.12
MESH = pl.DeviceIdType.MESH


def kernel(
    count,
    tracers,
    diffusivity,
    conductance,
    velocity,
    partner,
    weight,
    sea_mask,
    out,
    inflow_out,
    spare,
    lower,
    ratio,
    inverse,
    speed,
    keep,
    east,
    west,
    from_left,
    from_right,
    speed_left,
    mask_own,
    mask_left,
    mask_right,
    terms,
    wide,
    partner_own,
    weight_own,
    response,
    response_edge,
    inflow_edge,
    load_sem,
    tracer_sem,
    misc_send,
    misc_recv,
    edge_send,
    edge_recv,
    reply_send,
    reply_recv,
):
    _, trac, lev, width, rows = out.shape
    field = out.at[0]
    inflow = inflow_out.at[0]
    fields = (field, spare)
    chunks = lev // CHUNK
    component = lax.axis_index("mp")
    tile = lax.axis_index("tile")
    other = 1 - component
    right = lax.rem(tile + 1, count)
    left = lax.rem(tile + count - 1, count)
    half = width // 2

    def chunk_load(c):
        part = pl.ds(c * CHUNK, CHUNK)
        return pltpu.make_async_copy(tracers.at[0, :, part], field.at[:, part], tracer_sem.at[c])

    loads = [
        pltpu.make_async_copy(source, target, load_sem.at[i])
        for i, (source, target) in enumerate(
            [
                (diffusivity.at[0], lower.at[pl.ds(0, lev - 1)]),
                (conductance.at[0], terms.at[trac + 1]),
                (sea_mask, mask_own),
                (velocity.at[0], speed),
                (partner.at[0], partner_own),
                (weight.at[0], weight_own),
            ]
        )
    ]
    loads[0].start()
    for c in range(chunks):
        chunk_load(c).start()
    for load in loads[1:]:
        load.start()

    barrier = pltpu.get_barrier_semaphore()
    peers = [(component, left), (component, right), (other, tile), (other, left), (other, right)]
    for peer in peers:
        pl.semaphore_signal(barrier, inc=1, device_id=peer, device_id_type=MESH)
    pl.semaphore_wait(barrier, len(peers))

    def send(index, source, target, peer):
        return pltpu.make_async_remote_copy(
            src_ref=source,
            dst_ref=target,
            send_sem=misc_send.at[index],
            recv_sem=misc_recv.at[index],
            device_id=peer,
            device_id_type=MESH,
        )

    early = [
        send(0, velocity.at[0, :, width - 1], speed_left, (component, right)),
        send(1, sea_mask.at[pl.ds(half, half)], mask_left, (component, right)),
        send(2, sea_mask.at[pl.ds(0, half)], mask_right, (component, left)),
    ]

    def exchange_of(base, begin, size):
        ch = pl.ds(begin, size)
        moves = [
            (pl.ds(0, width), pl.ds(width, width), tile),
            (pl.ds(half, half), pl.ds(half, half), right),
            (half - 1, half - 1, right),
            (pl.ds(0, half), pl.ds(2 * width, half), left),
            (half, 2 * width + half, left),
        ]
        return [
            send(base + i, terms.at[ch, mine], wide.at[ch, theirs], (other, peer))
            for i, (mine, theirs, peer) in enumerate(moves)
        ]

    exchange_late = exchange_of(3, 0, trac)
    exchange_early = exchange_of(8, trac, 2)
    exchange = exchange_late + exchange_early
    for copy in early:
        copy.start()

    def edges(s, c, source=None):
        part = pl.ds(c * CHUNK, CHUNK)
        source = fields[s % 2] if source is None else source
        return [
            pltpu.make_async_remote_copy(
                src_ref=source.at[:, part, column],
                dst_ref=target.at[s, c],
                send_sem=edge_send.at[side, s, c],
                recv_sem=edge_recv.at[side, s, c],
                device_id=(component, peer),
                device_id_type=MESH,
            )
            for side, (column, target, peer) in enumerate(
                [(width - 1, from_left, right), (0, from_right, left)]
            )
        ]

    sides = [(width - 1, right), (0, left)]

    def replies(i):
        return [
            pltpu.make_async_remote_copy(
                src_ref=response.at[i, :, column],
                dst_ref=response_edge.at[side, i],
                send_sem=reply_send.at[side, i],
                recv_sem=reply_recv.at[side, i],
                device_id=(component, peer),
                device_id_type=MESH,
            )
            for side, (column, peer) in enumerate(sides)
        ]

    inflow_sends = [
        send(13 + side, inflow.at[:, column], inflow_edge.at[side], (component, peer))
        for side, (column, peer) in enumerate(sides)
    ]

    loads[0].wait()
    zero = jnp.zeros((width, rows), jnp.float32)
    lower[lev - 1] = zero

    def factor(l, carry):
        low, ratio_prev = carry
        high = lower[l]
        inv = 1.0 / (1.0 + low + high - low * ratio_prev)
        ratio_now = high * inv
        inverse[l] = inv
        lower[l] = low * inv
        ratio[l] = ratio_now
        return high, ratio_now

    lax.fori_loop(0, lev, factor, (zero, zero), unroll=4)
    slope = inverse[lev - 1]
    ratio[lev - 1] = slope
    terms[trac] = slope
    loads[1].wait()
    for copy in exchange_early:
        copy.start()

    def down_chunk(c, carry):
        chunk_load(c).wait()

        def down(k, partial):
            l = c * CHUNK + k
            low = lower[l]
            inv = inverse[l]
            now = tuple(field[t, l] * inv + low * partial[t] for t in range(trac))
            for t in range(trac):
                field[t, l] = now[t]
            return now

        return lax.fori_loop(0, CHUNK, down, carry, unroll=4)

    finals = lax.fori_loop(0, chunks, down_chunk, (zero,) * trac)
    for t in range(trac):
        terms[t] = finals[t]
    for copy in exchange_late:
        copy.start()

    def early_chunk(i, carry):
        c = chunks - 1 - i

        def up(k, above):
            l = c * CHUNK + CHUNK - 1 - k
            slant = ratio[l]
            now = tuple(field[t, l] + slant * above[t] for t in range(trac))
            for t in range(trac):
                spare[t, l] = now[t]
            reply = slant * above[trac]
            response[i, CHUNK - 1 - k] = reply
            return now + (reply,)

        carry = lax.fori_loop(0, CHUNK, up, carry, unroll=True)
        for copy in edges(0, c, spare) + replies(i):
            copy.start()
        return carry

    lax.fori_loop(0, EARLY, early_chunk, (zero,) * trac + (jnp.ones((width, rows), jnp.float32),))

    for load in loads[2:]:
        load.wait()
    for copy in exchange:
        copy.wait_recv()
    columns = count * width
    lanes = 128

    def surface(j, _):
        part = pl.ds(pl.multiple_of(j * lanes, lanes), lanes)
        for h in range(2):
            own_rows = pl.ds(h * half, half)
            place = tile * width + h * half + lax.broadcasted_iota(jnp.int32, (half, lanes), 0)
            own = [terms[ch, own_rows, part] for ch in range(trac + 2)]
            total = [jnp.zeros((half, lanes), jnp.float32) for _ in range(trac)]
            distance = [
                lax.rem(partner_own[k, own_rows, part] - place + (REACH + columns), columns)
                for k in range(2)
            ]
            peer = [[jnp.zeros((half, lanes), jnp.float32)] * (trac + 2) for k in range(2)]
            for offset in range(2 * REACH + 1):
                begin = width - REACH + offset + h * half
                hit = [distance[k] == offset for k in range(2)]
                for ch in range(trac + 2):
                    window = wide[ch, pl.ds(begin, half), part]
                    for k in range(2):
                        peer[k][ch] = jnp.where(hit[k], window, peer[k][ch])
            for k in range(2):
                series = own[trac + 1] * peer[k][trac + 1] / (own[trac + 1] + peer[k][trac + 1])
                scale = (
                    weight_own[k, own_rows, part].astype(jnp.float32)
                    * series
                    / (1.0 + series * (own[trac] + peer[k][trac]))
                )
                for t in range(trac):
                    total[t] = total[t] + scale * (own[t] - peer[k][t])
            for t in range(trac):
                inflow[t, own_rows, part] = total[t] * (-1.0 / QUANT)
        return 0

    lax.fori_loop(0, rows // lanes, surface, 0)

    for copy in inflow_sends:
        copy.start()

    def up_chunk(i, carry):
        c = chunks - 1 - i

        def up(k, above):
            l = c * CHUNK + CHUNK - 1 - k
            slant = ratio[l]
            now = tuple(field[t, l] + slant * above[t] for t in range(trac))
            for t in range(trac):
                field[t, l] = now[t]
            return now

        carry = lax.fori_loop(0, CHUNK, up, carry)

        @pl.when(i >= EARLY)
        def _():
            for copy in edges(0, c):
                copy.start()

        return carry

    lax.fori_loop(0, chunks, up_chunk, tuple(inflow[t] for t in range(trac)))

    for copy in early:
        copy.wait_recv()
    row = lax.broadcasted_iota(jnp.int32, (width, rows), 0)
    lane = lax.broadcasted_iota(jnp.int32, (width, rows), 1)
    first = row == 0
    last = row == width - 1

    def openness_of(mask):
        return jnp.where(component == 1, mask.astype(jnp.float32), jnp.ones(mask.shape, jnp.float32))

    openness = openness_of(mask_own[...])
    open_right = openness_of(mask_right[pl.ds(0, 1), :])
    open_left = openness_of(mask_left[pl.ds(half - 1, 1), :])
    open_east = openness * jnp.where(last, open_right, pltpu.roll(openness, width - 1, 0))
    open_west = openness * jnp.where(first, open_left, pltpu.roll(openness, 1, 0))
    north = jnp.where(lane == rows - 1, 0.0, diffusion_nu * openness * pltpu.roll(openness, rows - 1, 1))
    south = jnp.where(lane == 0, 0.0, diffusion_nu * openness * pltpu.roll(openness, 1, 1))

    def coefficients(l, _):
        here = speed[l]
        before = jnp.where(first, speed_left[pl.ds(l, 1), :], pltpu.roll(here, 1, 0))
        keep[l] = (
            1.0
            - north
            - south
            - open_east * (jnp.maximum(here, 0.0) + diffusion_nu)
            + open_west * (jnp.minimum(before, 0.0) - diffusion_nu)
        )
        east[l] = open_east * (diffusion_nu - jnp.minimum(here, 0.0))
        west[l] = open_west * (jnp.maximum(before, 0.0) + diffusion_nu)
        return 0

    lax.fori_loop(0, lev, coefficients, 0)

    def step(s):
        source, target = fields[s % 2], fields[(s + 1) % 2]

        def unit(i, _):
            c = chunks - 1 - i
            if s == 1:

                @pl.when(i >= EARLY)
                def _():
                    for copy in edges(0, c):
                        copy.wait_send()

            if s > 1:
                for copy in edges(s - 1, c):
                    copy.wait_send()
            for copy in edges(s, c):
                copy.wait_recv()
            if s == 0:

                @pl.when(i == 0)
                def _():
                    for copy in inflow_sends:
                        copy.wait_recv()

                @pl.when(i < EARLY)
                def _():
                    for copy in edges(0, c, spare) + replies(i):
                        copy.wait_send()
                    for copy in replies(i):
                        copy.wait_recv()
                    for side, edge in enumerate((from_left, from_right)):
                        for t in range(trac):
                            edge[0, c, t] = edge[0, c, t] + response_edge[side, i] * inflow_edge[side, pl.ds(t, 1), :]


            def level(k, _):
                l = c * CHUNK + k
                keep_l = keep[l]
                east_l = east[l]
                west_l = west[l]
                for t in range(trac):
                    here = source[t, l]
                    after = jnp.where(last, from_right[s, c, t, pl.ds(k, 1), :], pltpu.roll(here, width - 1, 0))
                    before = jnp.where(first, from_left[s, c, t, pl.ds(k, 1), :], pltpu.roll(here, 1, 0))
                    target[t, l] = (
                        keep_l * here
                        + east_l * after
                        + west_l * before
                        + north * pltpu.roll(here, rows - 1, 1)
                        + south * pltpu.roll(here, 1, 1)
                    )
                return 0

            lax.fori_loop(0, CHUNK, level, 0, unroll=True)
            if s < STEPS - 1:
                for copy in edges(s + 1, c):
                    copy.start()
            return 0

        lax.fori_loop(0, chunks, unit, 0)

    for s in range(STEPS):
        step(s)

    for c in range(chunks):
        for copy in edges(STEPS - 1, c):
            copy.wait_send()
    for copy in early + exchange + inflow_sends:
        copy.wait_send()


def write_back(value, inflow, value_out, inflow_out, sem):
    levels = value.shape[2] // 4
    copies = [pltpu.make_async_copy(inflow, inflow_out, sem.at[4])]
    for i in range(4):
        part = pl.ds(i * levels, levels)
        copies.append(pltpu.make_async_copy(value.at[:, :, part], value_out.at[:, :, part], sem.at[i]))
    for copy in copies:
        copy.start()
    for copy in copies:
        copy.wait()


def per_device(count, tracers, diffusivity, conductance, face_velocity, partner, weight, sea_mask):
    _, trac, lev, width, rows = tracers.shape
    chunks = lev // CHUNK
    full = (lev, width, rows)
    flat = (width, rows)
    anywhere = pl.BlockSpec(memory_space=pltpu.HBM)
    edge = (STEPS, chunks, trac, CHUNK, rows)
    dma = pltpu.SemaphoreType.DMA
    real = jnp.float32
    shapes = (
        jax.ShapeDtypeStruct(tracers.shape, real),
        jax.ShapeDtypeStruct((1, trac, width, rows), real),
    )
    vmem = pl.BlockSpec(memory_space=pltpu.VMEM)
    results = pl.pallas_call(
        functools.partial(kernel, count),
        out_shape=shapes,
        in_specs=[anywhere] * 7,
        out_specs=(vmem, vmem),
        scratch_shapes=[
            pltpu.VMEM((trac,) + full, real),
            pltpu.VMEM(full, real),
            pltpu.VMEM(full, real),
            pltpu.VMEM(full, real),
            pltpu.VMEM(full, real),
            pltpu.VMEM(full, real),
            pltpu.VMEM(full, real),
            pltpu.VMEM(full, real),
            pltpu.VMEM(edge, real),
            pltpu.VMEM(edge, real),
            pltpu.VMEM((lev, rows), real),
            pltpu.VMEM(flat, jnp.int32),
            pltpu.VMEM((width // 2, rows), jnp.int32),
            pltpu.VMEM((width // 2, rows), jnp.int32),
            pltpu.VMEM((trac + 2,) + flat, real),
            pltpu.VMEM((trac + 2, 3 * width, rows), real),
            pltpu.VMEM((2,) + flat, jnp.int32),
            pltpu.VMEM((2,) + flat, jnp.int32),
            pltpu.VMEM((EARLY, CHUNK) + flat, real),
            pltpu.VMEM((2, EARLY, CHUNK, rows), real),
            pltpu.VMEM((2, trac, rows), real),
            dma((6,)),
            dma((chunks,)),
            dma((15,)),
            dma((15,)),
            dma((2, STEPS, chunks)),
            dma((2, STEPS, chunks)),
            dma((2, EARLY)),
            dma((2, EARLY)),
        ],
        compiler_params=pltpu.CompilerParams(
            collective_id=0, has_side_effects=True, vmem_limit_bytes=34 * 1024 * 1024
        ),
        name="coupled_step",
    )(*[pltpu.with_memory_space_constraint(a, pltpu.HBM) for a in (tracers, diffusivity, conductance, face_velocity, partner, weight, sea_mask)])
    return pl.pallas_call(
        write_back,
        out_shape=shapes,
        in_specs=[vmem, vmem],
        out_specs=(anywhere, anywhere),
        scratch_shapes=[dma((5,))],
        compiler_params=pltpu.CompilerParams(vmem_limit_bytes=1024 * 1024),
        name="write_back",
    )(*results)


def solution(mesh):
    in_specs = (
        P("mp", None, None, "tile", None),
        P("mp", None, "tile", None),
        P("mp", "tile", None),
        P("mp", None, "tile", None),
        P("mp", None, "tile", None),
        P("mp", None, "tile", None),
        P("tile", None),
    )
    out_specs = (P("mp", None, None, "tile", None), P("mp", None, "tile", None))
    return jax.shard_map(
        functools.partial(per_device, mesh.shape["tile"]),
        mesh=mesh,
        in_specs=in_specs,
        out_specs=out_specs,
        check_vma=False,
    )
```
